32 devices in a mesh: dp: 16 (over z, x, core), tensor: 2 (over y).
Axes of the slice: x: 2, y: 2, z: 4, core: 2. Of those that a mesh axis runs over, the one named last changes fastest.
Arguments:
- frames: bfloat16 [16, 1500, 1280], P('dp', 'tensor'), may hold values from -6 to 6
- frame_counts: int32 [16], P('dp'), may hold values from 2 to 1500
- encoder_gain: float32 [1280], replicated, may hold values from 0.25 to 1.75
- encoder_shift: float32 [1280], replicated, may hold values from -3 to 3
- encoder_qkv: bfloat16 [3, 1280, 640], P(None, 'dp', 'tensor'), may hold values from -0.25 to 0.25
- encoder_out: bfloat16 [640, 1280], P('tensor', 'dp'), may hold values from -0.25 to 0.25
- post_gain: float32 [1280], replicated, may hold values from 0.25 to 1.75
- post_shift: float32 [1280], replicated, may hold values from -3 to 3
- projector: bfloat16 [1280, 2048], P('dp', 'tensor'), may hold values from -0.15625 to 0.15625
- projector_shift: float32 [2048], replicated, may hold values from -3 to 3
- text_embed: bfloat16 [16, 42, 2048], P('dp', 'tensor'), may hold values from -6 to 6
- decoder_gain: float32 [2048], replicated, may hold values from 0.25 to 1.75
- decoder_qkv: bfloat16 [3, 2048, 2048], P(None, 'dp', 'tensor'), may hold values from -0.25 to 0.25
- adapter_in: float32 [2, 2048, 64], replicated, may hold values from -0.125 to 0.125
- adapter_out: float32 [2, 64, 2048], P(None, None, 'tensor'), may hold values from -0.75 to 0.75
- audio_upstream: bfloat16 [16, 750, 2048], P('dp', None, 'tensor'), may hold values from -0.29882812 to 0.29882812
- text_upstream: bfloat16 [16, 42, 2048], P('dp', None, 'tensor'), may hold values from -0.29882812 to 0.29882812
Outputs:
- adapter_in_grad: float32 [2, 2048, 64], P(None, ('dp', 'tensor'))
- adapter_out_grad: float32 [2, 64, 2048], P(None, 'dp', 'tensor')
The draws below stay inside these ranges and needn't reach their ends.
All inputs are finite; a program needn't handle non-finite values.
Results may differ from the reference program's by a relative error of at most 0.034.
Values may be sent and summed in bfloat16 or wider, within the bound.
A program may use at most 128 MiB of HBM per device.

```python
import jax
import jax.numpy as jnp
from jax import lax

DE = 1280
EHD = 64
FRAMES = 1500
D = 2048
HD = 128
RANK = 64
TEXT = 42
EW = 640
HQ = 2048
AUDIO = 750
CLIPS = 16


def draw_frames(key, part):
    key = jax.random.fold_in(key, 1)
    noise_part = jax.random.normal(key, (CLIPS, FRAMES, DE), jnp.float32)
    result_rows = noise_part
    return jnp.clip(result_rows, -6.0, 6.0).astype(jnp.bfloat16)


def draw_text_embed(key, part):
    key = jax.random.fold_in(key, 3)
    noise_part = jax.random.normal(key, (CLIPS, TEXT, D), jnp.float32)
    result_rows = noise_part
    return jnp.clip(result_rows, -6.0, 6.0).astype(jnp.bfloat16)


def draw_encoder_qkv(key, part):
    key = jax.random.fold_in(key, 2)
    entries = jnp.clip(jax.random.normal(key, (3, DE, EW), jnp.float32), -6.0, 6.0) * DE ** (-0.5)
    return jnp.clip(entries, -0.25, 0.25).astype(jnp.bfloat16)


def draw_decoder_qkv(key, part):
    key = jax.random.fold_in(key, 4)
    entries = jnp.clip(jax.random.normal(key, (3, D, HQ), jnp.float32), -6.0, 6.0) * D ** (-0.5)
    return jnp.clip(entries, -0.25, 0.25).astype(jnp.bfloat16)


def touch_ends(values, key, least, largest):
    extent = values.shape
    spot = [jax.random.randint(jax.random.fold_in(key, axis), (), 0, extent[axis]) for axis in range(len(extent))]
    values = values.at[tuple(spot)].set(least)
    longest = extent.index(max(extent))
    spot[longest] = (spot[longest] + 1) % extent[longest]
    return values.at[tuple(spot)].set(largest)


def block_levels(key, dims, pieces, least, top_value):
    def one(axis_at, blocks):
        draws = jax.random.uniform(jax.random.fold_in(jax.random.fold_in(key, 6), axis_at), (blocks,), jnp.float32, least / len(pieces), top_value / len(pieces))
        return jnp.repeat(jnp.exp(draws), dims[axis_at] // blocks).reshape((-1,) + (1,) * (len(dims) - axis_at - 1))

    level = one(*pieces[0])
    for cut in pieces[1:]:
        level = level * one(*cut)
    return level


def noise(stream_key, dims, scale, bound, split=(), kind=jnp.bfloat16):
    level = block_levels(stream_key, dims, split, -0.22, 0.18) if split else 1.0
    result = jax.random.normal(stream_key, dims, jnp.float32) * scale * level
    return jnp.minimum(jnp.maximum(result, -bound), bound).astype(kind)


def setup_inputs(seed: int = 0) -> dict:
    keys = jax.random.split(jax.random.key(seed), 18)
    frames = draw_frames(jax.random.fold_in(keys[17], 71), 0)
    frame_counts = touch_ends(jax.random.randint(keys[1], (CLIPS,), 2, FRAMES + 1), jax.random.fold_in(keys[1], 1), 2, FRAMES).astype(jnp.int32)
    encoder_gain = jnp.clip(1.0 + 0.15 * jax.random.normal(keys[2], (DE,), jnp.float32), 0.25, 1.75)
    encoder_shift = noise(keys[3], (DE,), 0.5, 3.0, (), jnp.float32)
    encoder_qkv = draw_encoder_qkv(jax.random.fold_in(keys[17], 71), 0)
    encoder_out = noise(keys[5], (EW, DE), EW ** -0.5, 0.25, ((0, 2), (1, 16)))
    post_gain = jnp.clip(1.0 + 0.15 * jax.random.normal(keys[6], (DE,), jnp.float32), 0.25, 1.75)
    post_shift = noise(keys[7], (DE,), 0.5, 3.0, (), jnp.float32)
    projector = noise(keys[8], (DE, D), DE ** -0.5, 0.15625, ((0, 16), (1, 2)))
    projector_shift = noise(keys[9], (D,), 0.5, 3.0, (), jnp.float32)
    text_embed = draw_text_embed(jax.random.fold_in(keys[17], 71), 0)
    decoder_gain = jnp.clip(1.0 + 0.15 * jax.random.normal(keys[11], (D,), jnp.float32), 0.25, 1.75)
    decoder_qkv = draw_decoder_qkv(jax.random.fold_in(keys[17], 71), 0)
    adapter_in = noise(keys[13], (2, D, RANK), D ** -0.5, 0.125, (), jnp.float32)
    adapter_out = noise(keys[14], (2, RANK, HQ), RANK ** -0.5, 0.75, ((2, 2),), jnp.float32)
    audio_upstream = noise(keys[15], (CLIPS, AUDIO, HQ), 0.05, 0.29882812, ((0, 16), (2, 2)))
    text_upstream = noise(keys[16], (CLIPS, TEXT, HQ), 0.05, 0.29882812, ((0, 16), (2, 2)))
    return {"frames": frames, "frame_counts": frame_counts, "encoder_gain": encoder_gain, "encoder_shift": encoder_shift, "encoder_qkv": encoder_qkv, "encoder_out": encoder_out, "post_gain": post_gain, "post_shift": post_shift, "projector": projector, "projector_shift": projector_shift, "text_embed": text_embed, "decoder_gain": decoder_gain, "decoder_qkv": decoder_qkv, "adapter_in": adapter_in, "adapter_out": adapter_out, "audio_upstream": audio_upstream, "text_upstream": text_upstream}


EPS_LAYER = 1e-05
EPS_ROOT = 1e-06
ADAPTER_SCALE = 2.0
ROPE_BASE = 10000.0
HIGHEST = lax.Precision.HIGHEST

def layer_norm(values, gain, shift):
    values = values.astype(jnp.float32)
    center = values - lax.optimization_barrier(jnp.mean(values, -1, keepdims=True))
    spread = lax.optimization_barrier(jnp.mean(center * center, -1, keepdims=True))
    return center * lax.rsqrt(spread + EPS_LAYER) * gain + shift

def root_norm(values, gain):
    values = values.astype(jnp.float32)
    return (values * lax.rsqrt(lax.optimization_barrier(jnp.mean(values * values, -1, keepdims=True)) + EPS_ROOT) * gain).astype(jnp.bfloat16)

def encoder_head(queries, keys_in, values_in, usable):
    scores = jnp.dot(queries, keys_in.T, preferred_element_type=jnp.float32) * queries.shape[-1] ** (-0.5)
    scores = jnp.where(usable[None, :], scores, -jnp.inf)
    row_top = lax.optimization_barrier(jnp.max(scores, -1, keepdims=True))
    weights = jnp.exp(scores - row_top)
    probabilities = (weights / lax.optimization_barrier(jnp.sum(weights, -1, keepdims=True))).astype(jnp.bfloat16)
    return jnp.dot(probabilities, values_in, preferred_element_type=jnp.float32).astype(jnp.bfloat16)

def encoder_attention(queries, keys_in, values_in, usable, head_width):
    length = queries.shape[0]

    def heads_first(array_in):
        return array_in.reshape(array_in.shape[0], -1, head_width).transpose(1, 0, 2)
    context = lax.map(lambda members: encoder_head(members[0], members[1], members[2], usable), (heads_first(queries), heads_first(keys_in), heads_first(values_in)))
    return context.transpose(1, 0, 2).reshape(length, -1)

def rope_tables(length, head_width):
    position = jnp.arange(length).astype(jnp.float32)
    frequency = ROPE_BASE ** (-jnp.arange(0, head_width, 2).astype(jnp.float32) / head_width)
    angles = position[:, None] * frequency[None, :]
    angles = jnp.concatenate([angles, angles], -1)
    return (jnp.cos(angles)[:, None, :], jnp.sin(angles)[:, None, :])

def rotate(values, cosine, sine_table):
    half_width = values.shape[-1] // 2
    turned = jnp.concatenate([-values[..., half_width:], values[..., :half_width]], -1)
    return values * cosine + turned * sine_table

def unrotate(grad_rows, cosine, sine_table):
    half_width = grad_rows.shape[-1] // 2
    scaled = grad_rows * sine_table
    back_part = jnp.concatenate([scaled[..., half_width:], -scaled[..., :half_width]], -1)
    return grad_rows * cosine + back_part

def decoder_head(queries, keys_in, values_in, upstream, allowed):
    score_scale = queries.shape[-1] ** (-0.5)
    scores = jnp.dot(queries, keys_in.T, preferred_element_type=jnp.float32) * score_scale
    scores = jnp.where(allowed, scores, -jnp.inf)
    row_top = lax.optimization_barrier(jnp.max(scores, -1, keepdims=True))
    weights = jnp.exp(scores - row_top)
    probabilities = weights / lax.optimization_barrier(jnp.sum(weights, -1, keepdims=True))
    rounded = probabilities.astype(jnp.bfloat16)
    context = jnp.dot(rounded, values_in, preferred_element_type=jnp.float32).astype(jnp.bfloat16)
    row_delta = lax.optimization_barrier(jnp.sum(upstream.astype(jnp.float32) * context.astype(jnp.float32), -1, keepdims=True))
    grad_probs = jnp.dot(upstream, values_in.T, preferred_element_type=jnp.float32)
    grad_scores = (probabilities * (grad_probs - row_delta) * score_scale).astype(jnp.bfloat16)
    grad_query = jnp.dot(grad_scores, keys_in, preferred_element_type=jnp.float32)
    grad_value = jnp.dot(rounded.T, upstream, preferred_element_type=jnp.float32)
    return (grad_query, grad_value)

def adapter_grads(normed, query_base, key_base, value_base, upstream, frame_count, audio_total, adapter_in, adapter_out, head_width):
    length = normed.shape[0]
    full_rows = normed.astype(jnp.float32)
    low_query = jnp.dot(full_rows, adapter_in[0], precision=HIGHEST)
    low_value = jnp.dot(full_rows, adapter_in[1], precision=HIGHEST)
    queries = query_base + ADAPTER_SCALE * jnp.dot(low_query, adapter_out[0], precision=HIGHEST)
    values_in = value_base + ADAPTER_SCALE * jnp.dot(low_value, adapter_out[1], precision=HIGHEST)
    cosine, sine_table = rope_tables(length, head_width)
    queries = rotate(queries.reshape(length, -1, head_width), cosine, sine_table).astype(jnp.bfloat16)
    keys_in = rotate(key_base.reshape(length, -1, head_width), cosine, sine_table).astype(jnp.bfloat16)
    values_in = values_in.reshape(length, -1, head_width).astype(jnp.bfloat16)
    upstream = upstream.reshape(length, -1, head_width)
    position = jnp.arange(length, dtype=jnp.int32)
    key_usable = (position >= audio_total) | (position < (frame_count + 1) // 2)
    allowed = (position[None, :] <= position[:, None]) & key_usable[None, :]

    def heads_first(array_in):
        return array_in.transpose(1, 0, 2)
    grad_query, grad_value = lax.map(lambda members: decoder_head(members[0], members[1], members[2], members[3], allowed), (heads_first(queries), heads_first(keys_in), heads_first(values_in), heads_first(upstream)))
    grad_query = unrotate(heads_first(grad_query), cosine, sine_table).reshape(length, -1)
    grad_value = heads_first(grad_value).reshape(length, -1)
    grads_out = ADAPTER_SCALE * jnp.stack([jnp.dot(low_query.T, grad_query, precision=HIGHEST), jnp.dot(low_value.T, grad_value, precision=HIGHEST)])
    grads_in = ADAPTER_SCALE * jnp.stack([jnp.dot(full_rows.T, jnp.dot(grad_query, adapter_out[0].T, precision=HIGHEST), precision=HIGHEST), jnp.dot(full_rows.T, jnp.dot(grad_value, adapter_out[1].T, precision=HIGHEST), precision=HIGHEST)])
    return (grads_in, grads_out)

def reference(frames, frame_counts, encoder_gain, encoder_shift, encoder_qkv, encoder_out, post_gain, post_shift, projector, projector_shift, text_embed, decoder_gain, decoder_qkv, adapter_in, adapter_out, audio_upstream, text_upstream):

    def one_clip(members):
        frames_clip, frame_count, text_rows, audio_grad, text_grad = members
        normed_frames = layer_norm(frames_clip, encoder_gain, encoder_shift).astype(jnp.bfloat16)
        queries = jnp.dot(normed_frames, encoder_qkv[0], preferred_element_type=jnp.float32).astype(jnp.bfloat16)
        keys_in = jnp.dot(normed_frames, encoder_qkv[1], preferred_element_type=jnp.float32).astype(jnp.bfloat16)
        values_in = jnp.dot(normed_frames, encoder_qkv[2], preferred_element_type=jnp.float32).astype(jnp.bfloat16)
        position = jnp.arange(frames_clip.shape[0], dtype=jnp.int32)
        context = encoder_attention(queries, keys_in, values_in, position < frame_count, EHD)
        hidden = frames_clip.astype(jnp.float32) + jnp.dot(context, encoder_out, preferred_element_type=jnp.float32)
        pooled = lax.optimization_barrier(jnp.mean(hidden.reshape(-1, 2, hidden.shape[1]), 1))
        pooled_norm = layer_norm(pooled, post_gain, post_shift).astype(jnp.bfloat16)
        embedded = (jnp.dot(pooled_norm, projector, preferred_element_type=jnp.float32) + projector_shift).astype(jnp.bfloat16)
        sequence = jnp.concatenate([embedded, text_rows], 0)
        normed = root_norm(sequence, decoder_gain)
        query_base = jnp.dot(normed, decoder_qkv[0], preferred_element_type=jnp.float32)
        key_base = jnp.dot(normed, decoder_qkv[1], preferred_element_type=jnp.float32)
        value_base = jnp.dot(normed, decoder_qkv[2], preferred_element_type=jnp.float32)
        upstream = jnp.concatenate([audio_grad, text_grad], 0)
        return adapter_grads(normed, query_base, key_base, value_base, upstream, frame_count, embedded.shape[0], adapter_in, adapter_out, HD)
    grads_in, grads_out = lax.map(one_clip, (frames, frame_counts, text_embed, audio_upstream, text_upstream))
    return (lax.optimization_barrier(jnp.sum(grads_in, 0)), lax.optimization_barrier(jnp.sum(grads_out, 0)))
```

```python
import functools

import jax
import jax.numpy as jnp
from jax import lax
from jax.experimental import pallas as pl
from jax.experimental.pallas import tpu as pltpu
from jax.sharding import PartitionSpec as P

EHD = 64
HD = 128
RANK = 64

EPS_LAYER = 1e-05
EPS_ROOT = 1e-06
ADAPTER_SCALE = 2.0
ROPE_BASE = 10000.0
LOG2E = 1.4426950408889634
VMEM_BYTES = 56 * 1024 * 1024
F32 = jnp.float32
BF16 = jnp.bfloat16
MESH = pl.DeviceIdType.MESH


def round_up(value, unit):
    return -(-value // unit) * unit


def dot(a, b):
    return jnp.dot(a, b, preferred_element_type=F32)


def dot_t(a, b):
    return lax.dot_general(a, b, (((1,), (1,)), ((), ())), preferred_element_type=F32)


def dot_0(a, b):
    return lax.dot_general(a, b, (((0,), (0,)), ((), ())), preferred_element_type=F32)


def params():
    return pltpu.CompilerParams(vmem_limit_bytes=VMEM_BYTES)


def layer_norm(values, gain, shift):
    center = values - jnp.mean(values, -1, keepdims=True)
    spread = jnp.mean(center * center, -1, keepdims=True)
    return center * lax.rsqrt(spread + EPS_LAYER) * gain + shift


def pair_matrix(rows):
    row = lax.broadcasted_iota(jnp.int32, (rows // 2, rows), 0)
    col = lax.broadcasted_iota(jnp.int32, (rows // 2, rows), 1)
    return jnp.where((col == 2 * row) | (col == 2 * row + 1), 0.5, 0.0).astype(BF16)


def encode_kernel(length, frames, gain, shift, weights, triple, pooled):
    tile, width = frames.shape
    base = pl.program_id(0) * tile
    index = lax.broadcasted_iota(jnp.int32, (tile, 1), 0) + base
    rows = jnp.where(index < length, frames[...].astype(F32), 0.0)
    pooled[...] = dot(pair_matrix(tile), rows.astype(BF16))
    normed = layer_norm(rows, gain[...], shift[...]).astype(BF16)
    for j in range(3):
        triple[j] = dot(normed, weights[:, j].reshape(width, -1)).astype(BF16)


def encode(frames, gain, shift, weights):
    length, width = frames.shape
    parts, _, depth, columns = weights.shape
    tile = 256
    padded = round_up(length, 2 * tile)
    whole = lambda shape: pl.BlockSpec(shape, lambda i: (0,) * len(shape))
    return pl.pallas_call(
        functools.partial(encode_kernel, length),
        grid=(padded // tile,),
        in_specs=[
            pl.BlockSpec((tile, width), lambda i: (i, 0)),
            whole((1, width)),
            whole((1, width)),
            whole((parts, 3, depth, columns)),
        ],
        out_specs=[
            pl.BlockSpec((3, tile, columns), lambda i: (0, i, 0)),
            pl.BlockSpec((tile // 2, width), lambda i: (i, 0)),
        ],
        out_shape=[
            jax.ShapeDtypeStruct((3, padded, columns), BF16),
            jax.ShapeDtypeStruct((padded // 2, width), F32),
        ],
        compiler_params=params(),
        cost_estimate=pl.CostEstimate(
            flops=6 * padded * width * columns, bytes_accessed=14 * 2**20, transcendentals=0
        ),
        name="encode",
    )(frames, gain[None], shift[None], weights)


def encoder_attention_kernel(count, queries, keys, values, out):
    tile, columns = queries.shape[1:]
    total = keys.shape[1]
    index = lax.broadcasted_iota(jnp.int32, (1, total), 1)
    bias = jnp.where(index < count[0], 0.0, -jnp.inf)
    pairs = pair_matrix(tile)
    for head in range(columns // EHD):
        span = slice(head * EHD, (head + 1) * EHD)
        scores = dot_t(queries[0, :, span], keys[0, :, span]) * (EHD**-0.5 * LOG2E) + bias
        weights = jnp.exp2(scores - jnp.max(scores, -1, keepdims=True))
        total_weight = jnp.sum(weights, -1, keepdims=True)
        context = dot(weights.astype(BF16), values[0, :, span]) / total_weight
        out[:, span] = dot(pairs, context.astype(BF16)).astype(BF16)


def encoder_attention(triple, count):
    _, padded, columns = triple.shape
    tile = 512
    return pl.pallas_call(
        encoder_attention_kernel,
        grid=(padded // tile,),
        in_specs=[
            pl.BlockSpec(memory_space=pltpu.SMEM),
            pl.BlockSpec((1, tile, columns), lambda i: (0, i, 0)),
            pl.BlockSpec((1, padded, columns), lambda i: (1, 0, 0)),
            pl.BlockSpec((1, padded, columns), lambda i: (2, 0, 0)),
        ],
        out_specs=pl.BlockSpec((tile // 2, columns), lambda i: (i, 0)),
        out_shape=jax.ShapeDtypeStruct((padded // 2, columns), BF16),
        compiler_params=params(),
        cost_estimate=pl.CostEstimate(
            flops=16 * padded * padded * columns,
            bytes_accessed=4 * 2**20,
            transcendentals=padded * padded * (columns // EHD),
        ),
        name="encoder_attention",
    )(count, triple, triple, triple)


def embed_kernel(
    audio, pooled, context_a, context_b, out_w, gain, shift, proj_a, proj_b, proj_shift,
    text, root_gain, low_w, normed_out, low_out,
):
    tile = pooled.shape[0]
    half = out_w.shape[0] // 2
    hidden = pooled[...] + dot(context_a[...], out_w[:half]) + dot(context_b[...], out_w[half:])
    pooled_norm = layer_norm(hidden, gain[...], shift[...]).astype(BF16)
    columns = proj_a.shape[1]
    first = (dot(pooled_norm, proj_a[...]) + proj_shift[:, :columns]).astype(BF16)
    second = (dot(pooled_norm, proj_b[...]) + proj_shift[:, columns:]).astype(BF16)
    embedded = jnp.concatenate([first, second], 1).astype(F32)
    index = lax.broadcasted_iota(jnp.int32, (tile, 1), 0) + pl.program_id(0) * tile
    rows = jnp.where(index < audio, embedded, text[...].astype(F32))
    scale = lax.rsqrt(jnp.mean(rows * rows, -1, keepdims=True) + EPS_ROOT)
    normed = (rows * scale * root_gain[...]).astype(BF16)
    normed_out[...] = normed
    low_out[...] = dot(normed, low_w[...]).astype(BF16)


def embed(audio, pooled, context_a, context_b, out_w, gain, shift, proj_a, proj_b, proj_shift,
          text, root_gain, low_w):
    total, features = text.shape
    width = pooled.shape[1]
    tile = 128
    last = pooled.shape[0] // tile - 1
    whole = lambda shape: pl.BlockSpec(shape, lambda i: (0,) * len(shape))
    held = lambda i: (jnp.minimum(i, last), 0)
    row = lambda i: (i, 0)
    return pl.pallas_call(
        functools.partial(embed_kernel, audio),
        grid=(total // tile,),
        in_specs=[
            pl.BlockSpec((tile, width), held),
            pl.BlockSpec((tile, context_a.shape[1]), held),
            pl.BlockSpec((tile, context_b.shape[1]), held),
            whole(out_w.shape),
            whole((1, width)),
            whole((1, width)),
            whole(proj_a.shape),
            whole(proj_b.shape),
            whole((1, features)),
            pl.BlockSpec((tile, features), row),
            whole((1, features)),
            whole(low_w.shape),
        ],
        out_specs=[
            pl.BlockSpec((tile, features), row),
            pl.BlockSpec((tile, low_w.shape[1]), row),
        ],
        out_shape=[
            jax.ShapeDtypeStruct((total, features), BF16),
            jax.ShapeDtypeStruct((total, low_w.shape[1]), BF16),
        ],
        compiler_params=params(),
        cost_estimate=pl.CostEstimate(
            flops=2 * total * width * features * 2, bytes_accessed=24 * 2**20, transcendentals=0
        ),
        name="embed",
    )(pooled, context_a, context_b, out_w, gain[None], shift[None], proj_a, proj_b,
      proj_shift[None], text, root_gain[None], low_w)


def decoder_kernel(
    audio, count, normed, low, weights, up_w, upstream, cosine, sine, grads_out, grads_in,
    terms, grad_value,
):
    total, features = normed.shape
    step = pl.program_id(0)
    depth = weights.shape[1] // 3
    columns = weights.shape[2]
    scale = HD**-0.5

    @pl.when(step == 0)
    def _():
        terms[...] = jnp.zeros_like(terms)

    rows = normed[...]
    base = [
        dot(rows, weights[:, j * depth:(j + 1) * depth].reshape(features, columns))
        for j in range(3)
    ]
    up_q = up_w[0].astype(BF16)
    up_v = up_w[1].astype(BF16)
    low_q = low[:, :RANK]
    low_v = low[:, RANK:]
    all_q = base[0] + ADAPTER_SCALE * dot(low_q, up_q)
    all_v = (base[2] + ADAPTER_SCALE * dot(low_v, up_v)).astype(BF16)
    cos_t = cosine[...]
    sin_t = sine[...]
    usable = (count[0] + 1) // 2
    block = 256
    for head in range(columns // HD):
        span = slice(head * HD, (head + 1) * HD)
        q = all_q[:, span]
        k = base[1][:, span]
        q = (q * cos_t + pltpu.roll(q, HD // 2, 1) * sin_t).astype(BF16)
        k = (k * cos_t + pltpu.roll(k, HD // 2, 1) * sin_t).astype(BF16)
        v = all_v[:, span]
        u = upstream[:, span]
        grad_value[...] = jnp.zeros_like(grad_value)
        pieces = []
        for start in range(0, total, block):
            stop = min(start + block, total)
            key = lax.broadcasted_iota(jnp.int32, (stop - start, stop), 1)
            query = lax.broadcasted_iota(jnp.int32, (stop - start, stop), 0) + start
            allowed = (key <= query) & ((key >= audio) | (key < usable))
            scores = dot_t(q[start:stop], k[:stop]) * (scale * LOG2E)
            scores = jnp.where(allowed, scores, -jnp.inf)
            w = jnp.exp2(scores - jnp.max(scores, -1, keepdims=True))
            over = 1.0 / jnp.sum(w, -1, keepdims=True)
            w16 = w.astype(BF16)
            context = (dot(w16, v[:stop]) * over).astype(BF16)
            ub = u[start:stop].astype(F32)
            delta = jnp.sum(ub * context.astype(F32), -1, keepdims=True) * over
            scaled = (ub * over).astype(BF16)
            grad_probs = dot_t(scaled, v[:stop])
            dscores = (w * (grad_probs - delta)).astype(BF16)
            pieces.append(dot(dscores, k[:stop]) * scale)
            grad_value[:stop] += dot_0(w16, scaled)
        gq = jnp.concatenate(pieces, 0)
        gq = (gq * cos_t - pltpu.roll(gq, HD // 2, 1) * sin_t).astype(BF16)
        gv = grad_value[...].astype(BF16)
        grads_out[0, :, span] = ADAPTER_SCALE * dot_0(low_q, gq)
        grads_out[1, :, span] = ADAPTER_SCALE * dot_0(low_v, gv)
        terms[:, :RANK] += dot_t(gq, up_q[:, span])
        terms[:, RANK:] += dot_t(gv, up_v[:, span])

    @pl.when(step == pl.num_programs(0) - 1)
    def _():
        grads_in[...] = ADAPTER_SCALE * dot_0(terms[...].astype(BF16), rows)


def decoder(audio, count, normed, low, weights, up_w, upstream, cosine, sine):
    total, features = normed.shape
    parts, deep, all_columns = weights.shape
    columns = 2 * HD
    whole = lambda shape: pl.BlockSpec(shape, lambda i: (0,) * len(shape))
    return pl.pallas_call(
        functools.partial(decoder_kernel, audio),
        grid=(all_columns // columns,),
        in_specs=[
            pl.BlockSpec(memory_space=pltpu.SMEM),
            whole((total, features)),
            whole((total, 2 * RANK)),
            pl.BlockSpec((parts, deep, columns), lambda i: (0, 0, i)),
            pl.BlockSpec((2, RANK, columns), lambda i: (0, 0, i)),
            pl.BlockSpec((total, columns), lambda i: (0, i)),
            whole((total, HD)),
            whole((total, HD)),
        ],
        out_specs=[
            pl.BlockSpec((2, RANK, columns), lambda i: (0, 0, i)),
            whole((2 * RANK, features)),
        ],
        out_shape=[
            jax.ShapeDtypeStruct((2, RANK, all_columns), F32),
            jax.ShapeDtypeStruct((2 * RANK, features), F32),
        ],
        scratch_shapes=[pltpu.VMEM((total, 2 * RANK), F32), pltpu.VMEM((total, HD), F32)],
        compiler_params=params(),
        cost_estimate=pl.CostEstimate(
            flops=2 * total * features * all_columns * 5,
            bytes_accessed=24 * 2**20,
            transcendentals=total * total * 8,
        ),
        name="decoder",
    )(count, normed, low, weights, up_w, upstream, cosine, sine)


def reduce_kernel(parts, shared, terms, out, landed, mine, theirs, send_sem, recv_sem, pair_sem):
    dp = lax.axis_index("dp")
    tensor = lax.axis_index("tensor")
    partner = (dp, 1 - tensor)
    barrier = pltpu.get_barrier_semaphore()
    for k in range(1, parts):
        pl.semaphore_signal(
            barrier, inc=1, device_id=(lax.rem(dp + k, parts), tensor), device_id_type=MESH
        )
    pl.semaphore_signal(barrier, inc=1, device_id=partner, device_id_type=MESH)
    pl.semaphore_wait(barrier, parts)
    copies = []
    for k in range(1, parts):
        peer = lax.rem(dp + k, parts)
        copy = pltpu.make_async_remote_copy(
            src_ref=terms.at[peer],
            dst_ref=landed.at[k - 1],
            send_sem=send_sem.at[k - 1],
            recv_sem=recv_sem.at[k - 1],
            device_id=(peer, tensor),
            device_id_type=MESH,
        )
        copy.start()
        copies.append(copy)
    total = terms[dp].astype(F32)
    for k, copy in enumerate(copies):
        copy.wait()
        total = total + landed[k].astype(F32)
    mine[...] = total[:shared]
    copy = pltpu.make_async_remote_copy(
        src_ref=mine, dst_ref=theirs, send_sem=pair_sem.at[0], recv_sem=pair_sem.at[1],
        device_id=partner, device_id_type=MESH,
    )
    copy.start()
    out[shared:] = total[shared:]
    copy.wait()
    out[:shared] = total[:shared] + theirs[...]


def reduce_terms(terms, shared):
    parts, rows, columns = terms.shape
    return pl.pallas_call(
        functools.partial(reduce_kernel, parts, shared),
        out_shape=jax.ShapeDtypeStruct((rows, columns), F32),
        in_specs=[pl.BlockSpec(memory_space=pltpu.VMEM)],
        out_specs=pl.BlockSpec(memory_space=pltpu.VMEM),
        scratch_shapes=[
            pltpu.VMEM((parts - 1, rows, columns), BF16),
            pltpu.VMEM((shared, columns), F32),
            pltpu.VMEM((shared, columns), F32),
            pltpu.SemaphoreType.DMA((parts - 1,)),
            pltpu.SemaphoreType.DMA((parts - 1,)),
            pltpu.SemaphoreType.DMA((2,)),
        ],
        compiler_params=pltpu.CompilerParams(
            collective_id=0, has_side_effects=True, vmem_limit_bytes=VMEM_BYTES
        ),
        name="reduce_terms",
    )(terms)


def rope_tables(length):
    position = jnp.arange(length).astype(F32)
    frequency = ROPE_BASE ** (-jnp.arange(0, HD, 2).astype(F32) / HD)
    angles = position[:, None] * frequency[None, :]
    cosine, sine = jnp.cos(angles), jnp.sin(angles)
    return jnp.concatenate([cosine, cosine], -1), jnp.concatenate([-sine, sine], -1)


def both(value, axis):
    other = lax.ppermute(value, "tensor", [(0, 1), (1, 0)])
    first = lax.axis_index("tensor") == 0
    return jnp.where(first, value, other), jnp.where(first, other, value)


def per_device(
    frames,
    frame_counts,
    encoder_gain,
    encoder_shift,
    encoder_qkv,
    encoder_out,
    post_gain,
    post_shift,
    projector,
    projector_shift,
    text_embed,
    decoder_gain,
    decoder_qkv,
    adapter_in,
    adapter_out,
    audio_upstream,
    text_upstream,
):
    parts = lax.axis_size("dp")
    encoder_w = lax.all_gather(encoder_qkv, "dp")
    audio, columns = audio_upstream.shape[1:]
    text_rows = text_upstream.shape[1]
    total = round_up(audio + text_rows, 128)
    tail = total - audio - text_rows

    all_frames = jnp.concatenate(both(frames[0], 0), 0)
    text = jnp.concatenate(both(text_embed[0], 0), 0)
    text = jnp.pad(text, ((audio, tail), (0, 0)))
    upstream = jnp.pad(
        jnp.concatenate([audio_upstream[0], text_upstream[0]], 0), ((0, tail), (0, 0))
    )
    deep = decoder_qkv.shape[1]
    flat = encoder_out.reshape(-1)
    flat = jnp.pad(flat, (0, round_up(flat.size, columns) - flat.size))
    late = jnp.concatenate([flat.reshape(-1, columns), projector], 0)
    encoder_w, late = lax.optimization_barrier((encoder_w, late))
    if encoder_w.shape[2] % 16:
        encoder_w = encoder_w.transpose(1, 0, 2, 3).reshape(1, 3, -1, encoder_w.shape[3])
    late = lax.all_gather(late, "dp")
    split = late.shape[1] - projector.shape[0]
    late, decoder_rows = lax.optimization_barrier(
        (late, decoder_qkv.reshape(3 * deep, columns))
    )
    decoder_w = lax.all_gather(decoder_rows, "dp")
    out_half = late[:, :split].reshape(parts, -1)[:, :encoder_out.size]
    out_half = out_half.reshape((parts,) + encoder_out.shape).transpose(1, 0, 2)
    out_w = jnp.concatenate(both(out_half.reshape(encoder_out.shape[0], -1), 0), 0)
    proj_a, proj_b = both(late[:, split:].reshape(-1, columns), 1)

    triple, pooled = encode(all_frames, encoder_gain, encoder_shift, encoder_w)
    context = encoder_attention(triple, frame_counts)
    context_a, context_b = both(context, 1)
    low_w = jnp.concatenate([adapter_in[0], adapter_in[1]], 1).astype(BF16)
    normed, low = embed(
        audio, pooled, context_a, context_b, out_w, post_gain, post_shift, proj_a, proj_b,
        projector_shift, text, decoder_gain, low_w,
    )
    cosine, sine = rope_tables(total)
    grads_out, grads_in = decoder(
        audio, frame_counts, normed, low, decoder_w, adapter_out, upstream, cosine, sine
    )
    share = grads_in.shape[1] // parts
    ranks = RANK // parts if RANK >= parts else 1
    packed_in = grads_in.reshape(2 * RANK, parts, share).transpose(1, 0, 2)
    packed_out = grads_out.reshape(2, parts, ranks, columns).transpose(1, 0, 2, 3)
    shared = 2 * RANK
    packed = jnp.concatenate(
        [packed_in.astype(BF16), packed_out.astype(BF16).reshape(parts, -1, share)], 1
    )
    summed = reduce_terms(packed, shared)
    half = share // lax.axis_size("tensor")
    part_in = lax.dynamic_slice_in_dim(summed[:shared], lax.axis_index("tensor") * half, half, 1)
    part_in = part_in.reshape(2, RANK, half).transpose(0, 2, 1)
    part_out = summed[shared:].reshape(2, ranks, columns)
    return (part_in, part_out)


def solution(mesh):
    in_specs = (
        P("dp", "tensor", None),
        P("dp"),
        P(),
        P(),
        P(None, "dp", "tensor"),
        P("tensor", "dp"),
        P(),
        P(),
        P("dp", "tensor"),
        P(),
        P("dp", "tensor", None),
        P(),
        P(None, "dp", "tensor"),
        P(),
        P(None, None, "tensor"),
        P("dp", None, "tensor"),
        P("dp", None, "tensor"),
    )
    out_specs = (P(None, ("dp", "tensor"), None), P(None, "dp", "tensor"))
    return jax.shard_map(
        per_device, mesh=mesh, in_specs=in_specs, out_specs=out_specs, check_vma=False
    )
```

```python
import functools

import jax
import jax.numpy as jnp
from jax import lax
from jax.experimental import pallas as pl
from jax.experimental.pallas import tpu as pltpu
from jax.sharding import PartitionSpec as P

EHD = 64
HD = 128
RANK = 64

EPS_LAYER = 1e-05
EPS_ROOT = 1e-06
ADAPTER_SCALE = 2.0
ROPE_BASE = 10000.0
LOG2E = 1.4426950408889634
VMEM_BYTES = 56 * 1024 * 1024
F32 = jnp.float32
BF16 = jnp.bfloat16
MESH = pl.DeviceIdType.MESH


def round_up(value, unit):
    return -(-value // unit) * unit


def dot(a, b):
    return jnp.dot(a, b, preferred_element_type=F32)


def dot_t(a, b):
    return lax.dot_general(a, b, (((1,), (1,)), ((), ())), preferred_element_type=F32)


def dot_0(a, b):
    return lax.dot_general(a, b, (((0,), (0,)), ((), ())), preferred_element_type=F32)


def params():
    return pltpu.CompilerParams(vmem_limit_bytes=VMEM_BYTES)


def layer_norm(values, gain, shift):
    center = values - jnp.mean(values, -1, keepdims=True)
    spread = jnp.mean(center * center, -1, keepdims=True)
    return center * lax.rsqrt(spread + EPS_LAYER) * gain + shift


def pair_matrix(rows):
    row = lax.broadcasted_iota(jnp.int32, (rows // 2, rows), 0)
    col = lax.broadcasted_iota(jnp.int32, (rows // 2, rows), 1)
    return jnp.where((col == 2 * row) | (col == 2 * row + 1), 0.5, 0.0).astype(BF16)


def encode_kernel(length, frames, gain, shift, weights, triple, pooled):
    tile, width = frames.shape
    base = pl.program_id(0) * tile
    index = lax.broadcasted_iota(jnp.int32, (tile, 1), 0) + base
    rows = jnp.where(index < length, frames[...].astype(F32), 0.0)
    pooled[...] = dot(pair_matrix(tile), rows.astype(BF16))
    normed = layer_norm(rows, gain[...], shift[...]).astype(BF16)
    for j in range(3):
        triple[j] = dot(normed, weights[:, j].reshape(width, -1)).astype(BF16)


def encode(frames, gain, shift, weights):
    length, width = frames.shape
    parts, _, depth, columns = weights.shape
    tile = 256
    padded = round_up(length, 2 * tile)
    whole = lambda shape: pl.BlockSpec(shape, lambda i: (0,) * len(shape))
    return pl.pallas_call(
        functools.partial(encode_kernel, length),
        grid=(padded // tile,),
        in_specs=[
            pl.BlockSpec((tile, width), lambda i: (i, 0)),
            whole((1, width)),
            whole((1, width)),
            whole((parts, 3, depth, columns)),
        ],
        out_specs=[
            pl.BlockSpec((3, tile, columns), lambda i: (0, i, 0)),
            pl.BlockSpec((tile // 2, width), lambda i: (i, 0)),
        ],
        out_shape=[
            jax.ShapeDtypeStruct((3, padded, columns), BF16),
            jax.ShapeDtypeStruct((padded // 2, width), F32),
        ],
        compiler_params=params(),
        cost_estimate=pl.CostEstimate(
            flops=6 * padded * width * columns, bytes_accessed=14 * 2**20, transcendentals=0
        ),
        name="encode",
    )(frames, gain[None], shift[None], weights)


def encoder_attention_kernel(count, queries, keys, values, out):
    tile, columns = queries.shape[1:]
    total = keys.shape[1]
    index = lax.broadcasted_iota(jnp.int32, (1, total), 1)
    bias = jnp.where(index < count[0], 0.0, -jnp.inf)
    pairs = pair_matrix(tile)
    for head in range(columns // EHD):
        span = slice(head * EHD, (head + 1) * EHD)
        scores = dot_t(queries[0, :, span], keys[0, :, span]) * (EHD**-0.5 * LOG2E) + bias
        weights = jnp.exp2(scores - jnp.max(scores, -1, keepdims=True))
        total_weight = jnp.sum(weights, -1, keepdims=True)
        context = dot(weights.astype(BF16), values[0, :, span]) / total_weight
        out[:, span] = dot(pairs, context.astype(BF16)).astype(BF16)


def encoder_attention(triple, count):
    _, padded, columns = triple.shape
    tile = 512
    return pl.pallas_call(
        encoder_attention_kernel,
        grid=(padded // tile,),
        in_specs=[
            pl.BlockSpec(memory_space=pltpu.SMEM),
            pl.BlockSpec((1, tile, columns), lambda i: (0, i, 0)),
            pl.BlockSpec((1, padded, columns), lambda i: (1, 0, 0)),
            pl.BlockSpec((1, padded, columns), lambda i: (2, 0, 0)),
        ],
        out_specs=pl.BlockSpec((tile // 2, columns), lambda i: (i, 0)),
        out_shape=jax.ShapeDtypeStruct((padded // 2, columns), BF16),
        compiler_params=params(),
        cost_estimate=pl.CostEstimate(
            flops=16 * padded * padded * columns,
            bytes_accessed=4 * 2**20,
            transcendentals=padded * padded * (columns // EHD),
        ),
        name="encoder_attention",
    )(count, triple, triple, triple)


def embed_kernel(
    audio, pooled, context_a, context_b, out_w, gain, shift, proj_a, proj_b, proj_shift,
    text, root_gain, low_w, normed_out, low_out,
):
    tile = pooled.shape[0]
    half = out_w.shape[0] // 2
    hidden = pooled[...] + dot(context_a[...], out_w[:half]) + dot(context_b[...], out_w[half:])
    pooled_norm = layer_norm(hidden, gain[...], shift[...]).astype(BF16)
    columns = proj_a.shape[1]
    first = (dot(pooled_norm, proj_a[...]) + proj_shift[:, :columns]).astype(BF16)
    second = (dot(pooled_norm, proj_b[...]) + proj_shift[:, columns:]).astype(BF16)
    embedded = jnp.concatenate([first, second], 1).astype(F32)
    index = lax.broadcasted_iota(jnp.int32, (tile, 1), 0) + pl.program_id(0) * tile
    rows = jnp.where(index < audio, embedded, text[...].astype(F32))
    scale = lax.rsqrt(jnp.mean(rows * rows, -1, keepdims=True) + EPS_ROOT)
    normed = (rows * scale * root_gain[...]).astype(BF16)
    normed_out[...] = normed
    low_out[...] = dot(normed, low_w[...]).astype(BF16)


def embed(audio, pooled, context_a, context_b, out_w, gain, shift, proj_a, proj_b, proj_shift,
          text, root_gain, low_w):
    total, features = text.shape
    width = pooled.shape[1]
    tile = 128
    last = pooled.shape[0] // tile - 1
    whole = lambda shape: pl.BlockSpec(shape, lambda i: (0,) * len(shape))
    held = lambda i: (jnp.minimum(i, last), 0)
    row = lambda i: (i, 0)
    return pl.pallas_call(
        functools.partial(embed_kernel, audio),
        grid=(total // tile,),
        in_specs=[
            pl.BlockSpec((tile, width), held),
            pl.BlockSpec((tile, context_a.shape[1]), held),
            pl.BlockSpec((tile, context_b.shape[1]), held),
            whole(out_w.shape),
            whole((1, width)),
            whole((1, width)),
            whole(proj_a.shape),
            whole(proj_b.shape),
            whole((1, features)),
            pl.BlockSpec((tile, features), row),
            whole((1, features)),
            whole(low_w.shape),
        ],
        out_specs=[
            pl.BlockSpec((tile, features), row),
            pl.BlockSpec((tile, low_w.shape[1]), row),
        ],
        out_shape=[
            jax.ShapeDtypeStruct((total, features), BF16),
            jax.ShapeDtypeStruct((total, low_w.shape[1]), BF16),
        ],
        compiler_params=params(),
        cost_estimate=pl.CostEstimate(
            flops=2 * total * width * features * 2, bytes_accessed=24 * 2**20, transcendentals=0
        ),
        name="embed",
    )(pooled, context_a, context_b, out_w, gain[None], shift[None], proj_a, proj_b,
      proj_shift[None], text, root_gain[None], low_w)


def decoder_kernel(
    audio, count, normed, low, weights, up_w, upstream, cosine, sine, grads_out, grads_in,
    terms, grad_value,
):
    total, features = normed.shape
    step = pl.program_id(0)
    depth = weights.shape[1] // 3
    columns = weights.shape[2]
    scale = HD**-0.5

    @pl.when(step == 0)
    def _():
        terms[...] = jnp.zeros_like(terms)

    rows = normed[...]
    base = [
        dot(rows, weights[:, j * depth:(j + 1) * depth].reshape(features, columns))
        for j in range(3)
    ]
    up_q = up_w[0].astype(BF16)
    up_v = up_w[1].astype(BF16)
    low_q = low[:, :RANK]
    low_v = low[:, RANK:]
    all_q = base[0] + ADAPTER_SCALE * dot(low_q, up_q)
    all_v = (base[2] + ADAPTER_SCALE * dot(low_v, up_v)).astype(BF16)
    cos_t = cosine[...]
    sin_t = sine[...]
    usable = (count[0] + 1) // 2
    block = 256
    for head in range(columns // HD):
        span = slice(head * HD, (head + 1) * HD)
        q = all_q[:, span]
        k = base[1][:, span]
        q = (q * cos_t + pltpu.roll(q, HD // 2, 1) * sin_t).astype(BF16)
        k = (k * cos_t + pltpu.roll(k, HD // 2, 1) * sin_t).astype(BF16)
        v = all_v[:, span]
        u = upstream[:, span]
        grad_value[...] = jnp.zeros_like(grad_value)
        pieces = []
        for start in range(0, total, block):
            stop = min(start + block, total)
            key = lax.broadcasted_iota(jnp.int32, (stop - start, stop), 1)
            query = lax.broadcasted_iota(jnp.int32, (stop - start, stop), 0) + start
            allowed = (key <= query) & ((key >= audio) | (key < usable))
            scores = dot_t(q[start:stop], k[:stop]) * (scale * LOG2E)
            scores = jnp.where(allowed, scores, -jnp.inf)
            w = jnp.exp2(scores - jnp.max(scores, -1, keepdims=True))
            over = 1.0 / jnp.sum(w, -1, keepdims=True)
            w16 = w.astype(BF16)
            context = (dot(w16, v[:stop]) * over).astype(BF16)
            ub = u[start:stop].astype(F32)
            delta = jnp.sum(ub * context.astype(F32), -1, keepdims=True) * over
            scaled = (ub * over).astype(BF16)
            grad_probs = dot_t(scaled, v[:stop])
            dscores = (w * (grad_probs - delta)).astype(BF16)
            pieces.append(dot(dscores, k[:stop]) * scale)
            grad_value[:stop] += dot_0(w16, scaled)
        gq = jnp.concatenate(pieces, 0)
        gq = (gq * cos_t - pltpu.roll(gq, HD // 2, 1) * sin_t).astype(BF16)
        gv = grad_value[...].astype(BF16)
        grads_out[0, :, span] = ADAPTER_SCALE * dot_0(low_q, gq)
        grads_out[1, :, span] = ADAPTER_SCALE * dot_0(low_v, gv)
        terms[:, :RANK] += dot_t(gq, up_q[:, span])
        terms[:, RANK:] += dot_t(gv, up_v[:, span])

    @pl.when(step == pl.num_programs(0) - 1)
    def _():
        grads_in[...] = ADAPTER_SCALE * dot_0(terms[...].astype(BF16), rows)


def decoder(audio, count, normed, low, weights, up_w, upstream, cosine, sine):
    total, features = normed.shape
    parts, deep, all_columns = weights.shape
    columns = 2 * HD
    whole = lambda shape: pl.BlockSpec(shape, lambda i: (0,) * len(shape))
    return pl.pallas_call(
        functools.partial(decoder_kernel, audio),
        grid=(all_columns // columns,),
        in_specs=[
            pl.BlockSpec(memory_space=pltpu.SMEM),
            whole((total, features)),
            whole((total, 2 * RANK)),
            pl.BlockSpec((parts, deep, columns), lambda i: (0, 0, i)),
            pl.BlockSpec((2, RANK, columns), lambda i: (0, 0, i)),
            pl.BlockSpec((total, columns), lambda i: (0, i)),
            whole((total, HD)),
            whole((total, HD)),
        ],
        out_specs=[
            pl.BlockSpec((2, RANK, columns), lambda i: (0, 0, i)),
            whole((2 * RANK, features)),
        ],
        out_shape=[
            jax.ShapeDtypeStruct((2, RANK, all_columns), F32),
            jax.ShapeDtypeStruct((2 * RANK, features), F32),
        ],
        scratch_shapes=[pltpu.VMEM((total, 2 * RANK), F32), pltpu.VMEM((total, HD), F32)],
        compiler_params=params(),
        cost_estimate=pl.CostEstimate(
            flops=2 * total * features * all_columns * 5,
            bytes_accessed=24 * 2**20,
            transcendentals=total * total * 8,
        ),
        name="decoder",
    )(count, normed, low, weights, up_w, upstream, cosine, sine)


def reduce_kernel(parts, shared, terms, out, landed, mine, theirs, send_sem, recv_sem, pair_sem):
    dp = lax.axis_index("dp")
    tensor = lax.axis_index("tensor")
    partner = (dp, 1 - tensor)
    barrier = pltpu.get_barrier_semaphore()
    for k in range(1, parts):
        pl.semaphore_signal(
            barrier, inc=1, device_id=(lax.rem(dp + k, parts), tensor), device_id_type=MESH
        )
    pl.semaphore_signal(barrier, inc=1, device_id=partner, device_id_type=MESH)
    pl.semaphore_wait(barrier, parts)
    copies = []
    for k in range(1, parts):
        peer = lax.rem(dp + k, parts)
        copy = pltpu.make_async_remote_copy(
            src_ref=terms.at[peer],
            dst_ref=landed.at[k - 1],
            send_sem=send_sem.at[k - 1],
            recv_sem=recv_sem.at[k - 1],
            device_id=(peer, tensor),
            device_id_type=MESH,
        )
        copy.start()
        copies.append(copy)
    total = terms[dp].astype(F32)
    for k, copy in enumerate(copies):
        copy.wait()
        total = total + landed[k].astype(F32)
    mine[...] = total[:shared]
    copy = pltpu.make_async_remote_copy(
        src_ref=mine, dst_ref=theirs, send_sem=pair_sem.at[0], recv_sem=pair_sem.at[1],
        device_id=partner, device_id_type=MESH,
    )
    copy.start()
    out[shared:] = total[shared:]
    copy.wait()
    out[:shared] = total[:shared] + theirs[...]


def reduce_terms(terms, shared):
    parts, rows, columns = terms.shape
    return pl.pallas_call(
        functools.partial(reduce_kernel, parts, shared),
        out_shape=jax.ShapeDtypeStruct((rows, columns), F32),
        in_specs=[pl.BlockSpec(memory_space=pltpu.VMEM)],
        out_specs=pl.BlockSpec(memory_space=pltpu.VMEM),
        scratch_shapes=[
            pltpu.VMEM((parts - 1, rows, columns), BF16),
            pltpu.VMEM((shared, columns), F32),
            pltpu.VMEM((shared, columns), F32),
            pltpu.SemaphoreType.DMA((parts - 1,)),
            pltpu.SemaphoreType.DMA((parts - 1,)),
            pltpu.SemaphoreType.DMA((2,)),
        ],
        compiler_params=pltpu.CompilerParams(
            collective_id=0, has_side_effects=True, vmem_limit_bytes=VMEM_BYTES
        ),
        name="reduce_terms",
    )(terms)


def rope_tables(length):
    position = jnp.arange(length).astype(F32)
    frequency = ROPE_BASE ** (-jnp.arange(0, HD, 2).astype(F32) / HD)
    angles = position[:, None] * frequency[None, :]
    cosine, sine = jnp.cos(angles), jnp.sin(angles)
    return jnp.concatenate([cosine, cosine], -1), jnp.concatenate([-sine, sine], -1)


def both(value, axis):
    other = lax.ppermute(value, "tensor", [(0, 1), (1, 0)])
    first = lax.axis_index("tensor") == 0
    return jnp.where(first, value, other), jnp.where(first, other, value)


def per_device(
    frames,
    frame_counts,
    encoder_gain,
    encoder_shift,
    encoder_qkv,
    encoder_out,
    post_gain,
    post_shift,
    projector,
    projector_shift,
    text_embed,
    decoder_gain,
    decoder_qkv,
    adapter_in,
    adapter_out,
    audio_upstream,
    text_upstream,
):
    parts = lax.axis_size("dp")
    encoder_w = lax.all_gather(encoder_qkv, "dp")
    audio, columns = audio_upstream.shape[1:]
    text_rows = text_upstream.shape[1]
    total = round_up(audio + text_rows, 128)
    tail = total - audio - text_rows

    all_frames = jnp.concatenate(both(frames[0], 0), 0)
    text = jnp.concatenate(both(text_embed[0], 0), 0)
    text = jnp.pad(text, ((audio, tail), (0, 0)))
    upstream = jnp.pad(
        jnp.concatenate([audio_upstream[0], text_upstream[0]], 0), ((0, tail), (0, 0))
    )
    deep = decoder_qkv.shape[1]
    flat = encoder_out.reshape(-1)
    flat = jnp.pad(flat, (0, round_up(flat.size, columns) - flat.size))
    late = jnp.concatenate([flat.reshape(-1, columns), projector], 0)
    all_frames, late = lax.optimization_barrier((all_frames, late))
    if encoder_w.shape[2] % 16:
        encoder_w = encoder_w.transpose(1, 0, 2, 3).reshape(1, 3, -1, encoder_w.shape[3])
    late = lax.all_gather(late, "dp")
    split = late.shape[1] - projector.shape[0]
    triple, pooled = encode(all_frames, encoder_gain, encoder_shift, encoder_w)
    triple, decoder_rows = lax.optimization_barrier(
        (triple, decoder_qkv.reshape(3 * deep, columns))
    )
    decoder_w = lax.all_gather(decoder_rows, "dp")
    context = encoder_attention(triple, frame_counts)
    out_half = late[:, :split].reshape(parts, -1)[:, :encoder_out.size]
    out_half = out_half.reshape((parts,) + encoder_out.shape).transpose(1, 0, 2)
    out_w = jnp.concatenate(both(out_half.reshape(encoder_out.shape[0], -1), 0), 0)
    proj_a, proj_b = both(late[:, split:].reshape(-1, columns), 1)
    context_a, context_b = both(context, 1)
    low_w = jnp.concatenate([adapter_in[0], adapter_in[1]], 1).astype(BF16)
    normed, low = embed(
        audio, pooled, context_a, context_b, out_w, post_gain, post_shift, proj_a, proj_b,
        projector_shift, text, decoder_gain, low_w,
    )
    cosine, sine = rope_tables(total)
    grads_out, grads_in = decoder(
        audio, frame_counts, normed, low, decoder_w, adapter_out, upstream, cosine, sine
    )
    share = grads_in.shape[1] // parts
    ranks = RANK // parts if RANK >= parts else 1
    packed_in = grads_in.reshape(2 * RANK, parts, share).transpose(1, 0, 2)
    packed_out = grads_out.reshape(2, parts, ranks, columns).transpose(1, 0, 2, 3)
    shared = 2 * RANK
    packed = jnp.concatenate(
        [packed_in.astype(BF16), packed_out.astype(BF16).reshape(parts, -1, share)], 1
    )
    summed = reduce_terms(packed, shared)
    half = share // lax.axis_size("tensor")
    part_in = lax.dynamic_slice_in_dim(summed[:shared], lax.axis_index("tensor") * half, half, 1)
    part_in = part_in.reshape(2, RANK, half).transpose(0, 2, 1)
    part_out = summed[shared:].reshape(2, ranks, columns)
    return (part_in, part_out)


def solution(mesh):
    in_specs = (
        P("dp", "tensor", None),
        P("dp"),
        P(),
        P(),
        P(None, "dp", "tensor"),
        P("tensor", "dp"),
        P(),
        P(),
        P("dp", "tensor"),
        P(),
        P("dp", "tensor", None),
        P(),
        P(None, "dp", "tensor"),
        P(),
        P(None, None, "tensor"),
        P("dp", None, "tensor"),
        P("dp", None, "tensor"),
    )
    out_specs = (P(None, ("dp", "tensor"), None), P(None, "dp", "tensor"))
    return jax.shard_map(
        per_device, mesh=mesh, in_specs=in_specs, out_specs=out_specs, check_vma=False
    )
```

```python
import functools

import jax
import jax.numpy as jnp
from jax import lax
from jax.experimental import pallas as pl
from jax.experimental.pallas import tpu as pltpu
from jax.sharding import PartitionSpec as P

EHD = 64
HD = 128
RANK = 64

EPS_LAYER = 1e-05
EPS_ROOT = 1e-06
ADAPTER_SCALE = 2.0
ROPE_BASE = 10000.0
LOG2E = 1.4426950408889634
VMEM_BYTES = 56 * 1024 * 1024
F32 = jnp.float32
BF16 = jnp.bfloat16
MESH = pl.DeviceIdType.MESH


def round_up(value, unit):
    return -(-value // unit) * unit


def dot(a, b):
    return jnp.dot(a, b, preferred_element_type=F32)


def dot_t(a, b):
    return lax.dot_general(a, b, (((1,), (1,)), ((), ())), preferred_element_type=F32)


def dot_0(a, b):
    return lax.dot_general(a, b, (((0,), (0,)), ((), ())), preferred_element_type=F32)


def params():
    return pltpu.CompilerParams(vmem_limit_bytes=VMEM_BYTES)


def layer_norm(values, gain, shift):
    center = values - jnp.mean(values, -1, keepdims=True)
    spread = jnp.mean(center * center, -1, keepdims=True)
    return center * lax.rsqrt(spread + EPS_LAYER) * gain + shift


def pair_matrix(rows):
    row = lax.broadcasted_iota(jnp.int32, (rows // 2, rows), 0)
    col = lax.broadcasted_iota(jnp.int32, (rows // 2, rows), 1)
    return jnp.where((col == 2 * row) | (col == 2 * row + 1), 0.5, 0.0).astype(BF16)


def encode_kernel(length, frames, gain, shift, weights, triple, pooled):
    tile, width = frames.shape
    base = pl.program_id(0) * tile
    index = lax.broadcasted_iota(jnp.int32, (tile, 1), 0) + base
    rows = jnp.where(index < length, frames[...].astype(F32), 0.0)
    pooled[...] = dot(pair_matrix(tile), rows.astype(BF16))
    normed = layer_norm(rows, gain[...], shift[...]).astype(BF16)
    for j in range(3):
        triple[j] = dot(normed, weights[:, j].reshape(width, -1)).astype(BF16)


def encode(frames, gain, shift, weights):
    length, width = frames.shape
    parts, _, depth, columns = weights.shape
    tile = 512
    padded = round_up(length, tile)
    whole = lambda shape: pl.BlockSpec(shape, lambda i: (0,) * len(shape))
    return pl.pallas_call(
        functools.partial(encode_kernel, length),
        grid=(padded // tile,),
        in_specs=[
            pl.BlockSpec((tile, width), lambda i: (i, 0)),
            whole((1, width)),
            whole((1, width)),
            whole((parts, 3, depth, columns)),
        ],
        out_specs=[
            pl.BlockSpec((3, tile, columns), lambda i: (0, i, 0)),
            pl.BlockSpec((tile // 2, width), lambda i: (i, 0)),
        ],
        out_shape=[
            jax.ShapeDtypeStruct((3, padded, columns), BF16),
            jax.ShapeDtypeStruct((padded // 2, width), F32),
        ],
        compiler_params=params(),
        cost_estimate=pl.CostEstimate(
            flops=6 * padded * width * columns, bytes_accessed=14 * 2**20, transcendentals=0
        ),
        name="encode",
    )(frames, gain[None], shift[None], weights)


def encoder_attention_kernel(count, queries, keys, values, out):
    tile, columns = queries.shape[1:]
    total = keys.shape[1]
    index = lax.broadcasted_iota(jnp.int32, (1, total), 1)
    bias = jnp.where(index < count[0], 0.0, -jnp.inf)
    pairs = pair_matrix(tile)
    for head in range(columns // EHD):
        span = slice(head * EHD, (head + 1) * EHD)
        scores = dot_t(queries[0, :, span], keys[0, :, span]) * (EHD**-0.5 * LOG2E) + bias
        weights = jnp.exp2(scores - jnp.max(scores, -1, keepdims=True))
        total_weight = jnp.sum(weights, -1, keepdims=True)
        context = dot(weights.astype(BF16), values[0, :, span]) / total_weight
        out[:, span] = dot(pairs, context.astype(BF16)).astype(BF16)


def encoder_attention(triple, count):
    _, padded, columns = triple.shape
    tile = 512
    return pl.pallas_call(
        encoder_attention_kernel,
        grid=(padded // tile,),
        in_specs=[
            pl.BlockSpec(memory_space=pltpu.SMEM),
            pl.BlockSpec((1, tile, columns), lambda i: (0, i, 0)),
            pl.BlockSpec((1, padded, columns), lambda i: (1, 0, 0)),
            pl.BlockSpec((1, padded, columns), lambda i: (2, 0, 0)),
        ],
        out_specs=pl.BlockSpec((tile // 2, columns), lambda i: (i, 0)),
        out_shape=jax.ShapeDtypeStruct((padded // 2, columns), BF16),
        compiler_params=params(),
        cost_estimate=pl.CostEstimate(
            flops=16 * padded * padded * columns,
            bytes_accessed=4 * 2**20,
            transcendentals=padded * padded * (columns // EHD),
        ),
        name="encoder_attention",
    )(count, triple, triple, triple)


def embed_kernel(
    audio, pooled, context_a, context_b, out_w, gain, shift, proj_a, proj_b, proj_shift,
    text, root_gain, low_w, normed_out, low_out,
):
    tile = pooled.shape[0]
    half = out_w.shape[0] // 2
    hidden = pooled[...] + dot(context_a[...], out_w[:half]) + dot(context_b[...], out_w[half:])
    pooled_norm = layer_norm(hidden, gain[...], shift[...]).astype(BF16)
    columns = proj_a.shape[1]
    first = (dot(pooled_norm, proj_a[...]) + proj_shift[:, :columns]).astype(BF16)
    second = (dot(pooled_norm, proj_b[...]) + proj_shift[:, columns:]).astype(BF16)
    embedded = jnp.concatenate([first, second], 1).astype(F32)
    index = lax.broadcasted_iota(jnp.int32, (tile, 1), 0) + pl.program_id(0) * tile
    rows = jnp.where(index < audio, embedded, text[...].astype(F32))
    scale = lax.rsqrt(jnp.mean(rows * rows, -1, keepdims=True) + EPS_ROOT)
    normed = (rows * scale * root_gain[...]).astype(BF16)
    normed_out[...] = normed
    low_out[...] = dot(normed, low_w[...]).astype(BF16)


def embed(audio, pooled, context_a, context_b, out_w, gain, shift, proj_a, proj_b, proj_shift,
          text, root_gain, low_w):
    total, features = text.shape
    width = pooled.shape[1]
    tile = total // 2
    last = -(-pooled.shape[0] // tile) - 1
    whole = lambda shape: pl.BlockSpec(shape, lambda i: (0,) * len(shape))
    held = lambda i: (jnp.minimum(i, last), 0)
    row = lambda i: (i, 0)
    return pl.pallas_call(
        functools.partial(embed_kernel, audio),
        grid=(total // tile,),
        in_specs=[
            pl.BlockSpec((tile, width), held),
            pl.BlockSpec((tile, context_a.shape[1]), held),
            pl.BlockSpec((tile, context_b.shape[1]), held),
            whole(out_w.shape),
            whole((1, width)),
            whole((1, width)),
            whole(proj_a.shape),
            whole(proj_b.shape),
            whole((1, features)),
            pl.BlockSpec((tile, features), row),
            whole((1, features)),
            whole(low_w.shape),
        ],
        out_specs=[
            pl.BlockSpec((tile, features), row),
            pl.BlockSpec((tile, low_w.shape[1]), row),
        ],
        out_shape=[
            jax.ShapeDtypeStruct((total, features), BF16),
            jax.ShapeDtypeStruct((total, low_w.shape[1]), BF16),
        ],
        compiler_params=params(),
        cost_estimate=pl.CostEstimate(
            flops=2 * total * width * features * 2, bytes_accessed=24 * 2**20, transcendentals=0
        ),
        name="embed",
    )(pooled, context_a, context_b, out_w, gain[None], shift[None], proj_a, proj_b,
      proj_shift[None], text, root_gain[None], low_w)


def decoder_kernel(
    audio, count, normed, low, weights, up_w, upstream, cosine, sine, grads_out, grads_in,
    terms, grad_value,
):
    total, features = normed.shape
    step = pl.program_id(0)
    depth = weights.shape[1] // 3
    columns = weights.shape[2]
    scale = HD**-0.5

    @pl.when(step == 0)
    def _():
        terms[...] = jnp.zeros_like(terms)

    rows = normed[...]
    base = [
        dot(rows, weights[:, j * depth:(j + 1) * depth].reshape(features, columns))
        for j in range(3)
    ]
    up_q = up_w[0].astype(BF16)
    up_v = up_w[1].astype(BF16)
    low_q = low[:, :RANK]
    low_v = low[:, RANK:]
    all_q = base[0] + ADAPTER_SCALE * dot(low_q, up_q)
    all_v = (base[2] + ADAPTER_SCALE * dot(low_v, up_v)).astype(BF16)
    cos_t = cosine[...]
    sin_t = sine[...]
    usable = (count[0] + 1) // 2
    block = 256
    for head in range(columns // HD):
        span = slice(head * HD, (head + 1) * HD)
        q = all_q[:, span]
        k = base[1][:, span]
        q = (q * cos_t + pltpu.roll(q, HD // 2, 1) * sin_t).astype(BF16)
        k = (k * cos_t + pltpu.roll(k, HD // 2, 1) * sin_t).astype(BF16)
        v = all_v[:, span]
        u = upstream[:, span]
        grad_value[...] = jnp.zeros_like(grad_value)
        pieces = []
        for start in range(0, total, block):
            stop = min(start + block, total)
            key = lax.broadcasted_iota(jnp.int32, (stop - start, stop), 1)
            query = lax.broadcasted_iota(jnp.int32, (stop - start, stop), 0) + start
            allowed = (key <= query) & ((key >= audio) | (key < usable))
            scores = dot_t(q[start:stop], k[:stop]) * (scale * LOG2E)
            scores = jnp.where(allowed, scores, -jnp.inf)
            w = jnp.exp2(scores - jnp.max(scores, -1, keepdims=True))
            over = 1.0 / jnp.sum(w, -1, keepdims=True)
            w16 = w.astype(BF16)
            context = (dot(w16, v[:stop]) * over).astype(BF16)
            ub = u[start:stop].astype(F32)
            delta = jnp.sum(ub * context.astype(F32), -1, keepdims=True) * over
            scaled = (ub * over).astype(BF16)
            grad_probs = dot_t(scaled, v[:stop])
            dscores = (w * (grad_probs - delta)).astype(BF16)
            pieces.append(dot(dscores, k[:stop]) * scale)
            grad_value[:stop] += dot_0(w16, scaled)
        gq = jnp.concatenate(pieces, 0)
        gq = (gq * cos_t - pltpu.roll(gq, HD // 2, 1) * sin_t).astype(BF16)
        gv = grad_value[...].astype(BF16)
        grads_out[0, :, span] = ADAPTER_SCALE * dot_0(low_q, gq)
        grads_out[1, :, span] = ADAPTER_SCALE * dot_0(low_v, gv)
        terms[:, :RANK] += dot_t(gq, up_q[:, span])
        terms[:, RANK:] += dot_t(gv, up_v[:, span])

    @pl.when(step == pl.num_programs(0) - 1)
    def _():
        grads_in[...] = ADAPTER_SCALE * dot_0(terms[...].astype(BF16), rows)


def decoder(audio, count, normed, low, weights, up_w, upstream, cosine, sine):
    total, features = normed.shape
    parts, deep, all_columns = weights.shape
    columns = 2 * HD
    whole = lambda shape: pl.BlockSpec(shape, lambda i: (0,) * len(shape))
    return pl.pallas_call(
        functools.partial(decoder_kernel, audio),
        grid=(all_columns // columns,),
        in_specs=[
            pl.BlockSpec(memory_space=pltpu.SMEM),
            whole((total, features)),
            whole((total, 2 * RANK)),
            pl.BlockSpec((parts, deep, columns), lambda i: (0, 0, i)),
            pl.BlockSpec((2, RANK, columns), lambda i: (0, 0, i)),
            pl.BlockSpec((total, columns), lambda i: (0, i)),
            whole((total, HD)),
            whole((total, HD)),
        ],
        out_specs=[
            pl.BlockSpec((2, RANK, columns), lambda i: (0, 0, i)),
            whole((2 * RANK, features)),
        ],
        out_shape=[
            jax.ShapeDtypeStruct((2, RANK, all_columns), F32),
            jax.ShapeDtypeStruct((2 * RANK, features), F32),
        ],
        scratch_shapes=[pltpu.VMEM((total, 2 * RANK), F32), pltpu.VMEM((total, HD), F32)],
        compiler_params=params(),
        cost_estimate=pl.CostEstimate(
            flops=2 * total * features * all_columns * 5,
            bytes_accessed=24 * 2**20,
            transcendentals=total * total * 8,
        ),
        name="decoder",
    )(count, normed, low, weights, up_w, upstream, cosine, sine)


def reduce_kernel(parts, shared, terms, out, landed, mine, theirs, send_sem, recv_sem, pair_sem):
    dp = lax.axis_index("dp")
    tensor = lax.axis_index("tensor")
    partner = (dp, 1 - tensor)
    barrier = pltpu.get_barrier_semaphore()
    for k in range(1, parts):
        pl.semaphore_signal(
            barrier, inc=1, device_id=(lax.rem(dp + k, parts), tensor), device_id_type=MESH
        )
    pl.semaphore_signal(barrier, inc=1, device_id=partner, device_id_type=MESH)
    pl.semaphore_wait(barrier, parts)
    copies = []
    for k in range(1, parts):
        peer = lax.rem(dp + k, parts)
        copy = pltpu.make_async_remote_copy(
            src_ref=terms.at[peer],
            dst_ref=landed.at[k - 1],
            send_sem=send_sem.at[k - 1],
            recv_sem=recv_sem.at[k - 1],
            device_id=(peer, tensor),
            device_id_type=MESH,
        )
        copy.start()
        copies.append(copy)
    total = terms[dp].astype(F32)
    for k, copy in enumerate(copies):
        copy.wait()
        total = total + landed[k].astype(F32)
    mine[...] = total[:shared]
    copy = pltpu.make_async_remote_copy(
        src_ref=mine, dst_ref=theirs, send_sem=pair_sem.at[0], recv_sem=pair_sem.at[1],
        device_id=partner, device_id_type=MESH,
    )
    copy.start()
    out[shared:] = total[shared:]
    copy.wait()
    out[:shared] = total[:shared] + theirs[...]


def reduce_terms(terms, shared):
    parts, rows, columns = terms.shape
    return pl.pallas_call(
        functools.partial(reduce_kernel, parts, shared),
        out_shape=jax.ShapeDtypeStruct((rows, columns), F32),
        in_specs=[pl.BlockSpec(memory_space=pltpu.VMEM)],
        out_specs=pl.BlockSpec(memory_space=pltpu.VMEM),
        scratch_shapes=[
            pltpu.VMEM((parts - 1, rows, columns), BF16),
            pltpu.VMEM((shared, columns), F32),
            pltpu.VMEM((shared, columns), F32),
            pltpu.SemaphoreType.DMA((parts - 1,)),
            pltpu.SemaphoreType.DMA((parts - 1,)),
            pltpu.SemaphoreType.DMA((2,)),
        ],
        compiler_params=pltpu.CompilerParams(
            collective_id=0, has_side_effects=True, vmem_limit_bytes=VMEM_BYTES
        ),
        name="reduce_terms",
    )(terms)


def ring_index(place, parts):
    half = parts // 2
    row = lax.div(place, half)
    step = place - row * half
    core = lax.rem(step, 2)
    level = lax.div(step, 2)
    level = (1 - row) * level + row * (parts // 4 - 1 - level)
    return level * 4 + row * 2 + core


def ring_place(index, parts):
    core = lax.rem(index, 2)
    row = lax.rem(lax.div(index, 2), 2)
    level = lax.div(index, 4)
    level = (1 - row) * level + row * (parts // 4 - 1 - level)
    return row * (parts // 2) + level * 2 + core


def ring_kernel(parts, count, *refs):
    shards, wholes = refs[:count], refs[count:2 * count]
    local_sem, send_sem, recv_sem = refs[2 * count:]
    me = lax.axis_index("dp")
    tensor = lax.axis_index("tensor")
    place = ring_place(me, parts)
    right = ring_index(lax.rem(place + 1, parts), parts)
    left = ring_index(lax.rem(place + parts - 1, parts), parts)
    barrier = pltpu.get_barrier_semaphore()
    for peer in (left, right):
        pl.semaphore_signal(barrier, inc=1, device_id=(peer, tensor), device_id_type=MESH)
    pl.semaphore_wait(barrier, 2)
    own = []
    for i in range(count):
        copy = pltpu.make_async_copy(shards[i], wholes[i].at[me], local_sem.at[i])
        copy.start()
        own.append(copy)
    sent = []
    before = {}
    ways = ((right, parts // 2, parts - 1), (left, parts - 1 - parts // 2, 1))
    for step in range(parts // 2):
        for i in range(count):
            for way, (peer, steps, turn) in enumerate(ways):
                if step >= steps:
                    continue
                if step > 0:
                    before[way, i].wait_recv()
                owner = ring_index(lax.rem(place + step * turn, parts), parts)
                copy = pltpu.make_async_remote_copy(
                    src_ref=shards[i] if step == 0 else wholes[i].at[owner],
                    dst_ref=wholes[i].at[owner],
                    send_sem=send_sem.at[way, step, i],
                    recv_sem=recv_sem.at[way, step, i],
                    device_id=(peer, tensor),
                    device_id_type=MESH,
                )
                copy.start()
                sent.append(copy)
                before[way, i] = copy
    for copy in before.values():
        copy.wait_recv()
    for copy in sent:
        copy.wait_send()
    for copy in own:
        copy.wait()


def ring_gather(shards):
    parts = lax.axis_size("dp")
    count = len(shards)
    anywhere = pl.BlockSpec(memory_space=pl.ANY)
    return pl.pallas_call(
        functools.partial(ring_kernel, parts, count),
        out_shape=[jax.ShapeDtypeStruct((parts,) + s.shape, s.dtype) for s in shards],
        in_specs=[anywhere] * count,
        out_specs=[anywhere] * count,
        scratch_shapes=[
            pltpu.SemaphoreType.DMA((count,)),
            pltpu.SemaphoreType.DMA((2, parts // 2, count)),
            pltpu.SemaphoreType.DMA((2, parts // 2, count)),
        ],
        compiler_params=pltpu.CompilerParams(
            collective_id=1, has_side_effects=True, vmem_limit_bytes=VMEM_BYTES
        ),
        cost_estimate=pl.CostEstimate(flops=0, bytes_accessed=128 * 2**20, transcendentals=0),
        name="ring_gather",
    )(*shards)


def rope_tables(length):
    position = jnp.arange(length).astype(F32)
    frequency = ROPE_BASE ** (-jnp.arange(0, HD, 2).astype(F32) / HD)
    angles = position[:, None] * frequency[None, :]
    cosine, sine = jnp.cos(angles), jnp.sin(angles)
    return jnp.concatenate([cosine, cosine], -1), jnp.concatenate([-sine, sine], -1)


def both(value, axis):
    other = lax.ppermute(value, "tensor", [(0, 1), (1, 0)])
    first = lax.axis_index("tensor") == 0
    return jnp.where(first, value, other), jnp.where(first, other, value)


def per_device(
    frames,
    frame_counts,
    encoder_gain,
    encoder_shift,
    encoder_qkv,
    encoder_out,
    post_gain,
    post_shift,
    projector,
    projector_shift,
    text_embed,
    decoder_gain,
    decoder_qkv,
    adapter_in,
    adapter_out,
    audio_upstream,
    text_upstream,
):
    parts = lax.axis_size("dp")
    audio, columns = audio_upstream.shape[1:]
    text_rows = text_upstream.shape[1]
    total = round_up(audio + text_rows, 128)
    tail = total - audio - text_rows
    deep = decoder_qkv.shape[1]

    decoder_w = lax.all_gather(decoder_qkv.reshape(3 * deep, columns), "dp")
    all_frames = jnp.concatenate(both(frames[0], 0), 0)
    shards = [encoder_qkv, encoder_out, projector]
    if parts % 4 == 0 and encoder_qkv.shape[1] % 16 == 0:
        encoder_w, out_parts, proj_parts = ring_gather(shards)
    else:
        encoder_w, out_parts, proj_parts = [lax.all_gather(s, "dp") for s in shards]
        encoder_w = encoder_w.transpose(1, 0, 2, 3).reshape(1, 3, -1, encoder_w.shape[3])
    out_half = out_parts.transpose(1, 0, 2).reshape(encoder_out.shape[0], -1)
    proj_a, proj_b = both(proj_parts.reshape(-1, columns), 1)
    out_w = jnp.concatenate(both(out_half, 0), 0)
    text = jnp.concatenate(both(text_embed[0], 0), 0)
    text = jnp.pad(text, ((audio, tail), (0, 0)))
    upstream = jnp.pad(
        jnp.concatenate([audio_upstream[0], text_upstream[0]], 0), ((0, tail), (0, 0))
    )
    triple, pooled = encode(all_frames, encoder_gain, encoder_shift, encoder_w)
    context = encoder_attention(triple, frame_counts)
    context_a, context_b = both(context, 1)
    low_w = jnp.concatenate([adapter_in[0], adapter_in[1]], 1).astype(BF16)
    normed, low = embed(
        audio, pooled, context_a, context_b, out_w, post_gain, post_shift, proj_a, proj_b,
        projector_shift, text, decoder_gain, low_w,
    )
    cosine, sine = rope_tables(total)
    grads_out, grads_in = decoder(
        audio, frame_counts, normed, low, decoder_w, adapter_out, upstream, cosine, sine
    )
    share = grads_in.shape[1] // parts
    ranks = RANK // parts if RANK >= parts else 1
    packed_in = grads_in.reshape(2 * RANK, parts, share).transpose(1, 0, 2)
    packed_out = grads_out.reshape(2, parts, ranks, columns).transpose(1, 0, 2, 3)
    shared = 2 * RANK
    packed = jnp.concatenate(
        [packed_in.astype(BF16), packed_out.astype(BF16).reshape(parts, -1, share)], 1
    )
    summed = reduce_terms(packed, shared)
    half = share // lax.axis_size("tensor")
    part_in = lax.dynamic_slice_in_dim(summed[:shared], lax.axis_index("tensor") * half, half, 1)
    part_in = part_in.reshape(2, RANK, half).transpose(0, 2, 1)
    part_out = summed[shared:].reshape(2, ranks, columns)
    return (part_in, part_out)


def solution(mesh):
    in_specs = (
        P("dp", "tensor", None),
        P("dp"),
        P(),
        P(),
        P(None, "dp", "tensor"),
        P("tensor", "dp"),
        P(),
        P(),
        P("dp", "tensor"),
        P(),
        P("dp", "tensor", None),
        P(),
        P(None, "dp", "tensor"),
        P(),
        P(None, None, "tensor"),
        P("dp", None, "tensor"),
        P("dp", None, "tensor"),
    )
    out_specs = (P(None, ("dp", "tensor"), None), P(None, "dp", "tensor"))
    return jax.shard_map(
        per_device, mesh=mesh, in_specs=in_specs, out_specs=out_specs, check_vma=False
    )
```

```python
import functools

import jax
import jax.numpy as jnp
from jax import lax
from jax.experimental import pallas as pl
from jax.experimental.pallas import tpu as pltpu
from jax.sharding import PartitionSpec as P

EHD = 64
HD = 128
RANK = 64

EPS_LAYER = 1e-05
EPS_ROOT = 1e-06
ADAPTER_SCALE = 2.0
ROPE_BASE = 10000.0
LOG2E = 1.4426950408889634
VMEM_BYTES = 56 * 1024 * 1024
F32 = jnp.float32
BF16 = jnp.bfloat16
MESH = pl.DeviceIdType.MESH


def round_up(value, unit):
    return -(-value // unit) * unit


def dot(a, b):
    return jnp.dot(a, b, preferred_element_type=F32)


def dot_t(a, b):
    return lax.dot_general(a, b, (((1,), (1,)), ((), ())), preferred_element_type=F32)


def dot_0(a, b):
    return lax.dot_general(a, b, (((0,), (0,)), ((), ())), preferred_element_type=F32)


def params():
    return pltpu.CompilerParams(vmem_limit_bytes=VMEM_BYTES)


def layer_norm(values, gain, shift):
    center = values - jnp.mean(values, -1, keepdims=True)
    spread = jnp.mean(center * center, -1, keepdims=True)
    return center * lax.rsqrt(spread + EPS_LAYER) * gain + shift


def pair_matrix(rows):
    row = lax.broadcasted_iota(jnp.int32, (rows // 2, rows), 0)
    col = lax.broadcasted_iota(jnp.int32, (rows // 2, rows), 1)
    return jnp.where((col == 2 * row) | (col == 2 * row + 1), 0.5, 0.0).astype(BF16)


def encode_kernel(length, frames, gain, shift, weights, triple, pooled):
    tile, width = frames.shape
    base = pl.program_id(0) * tile
    index = lax.broadcasted_iota(jnp.int32, (tile, 1), 0) + base
    rows = jnp.where(index < length, frames[...].astype(F32), 0.0)
    pooled[...] = dot(pair_matrix(tile), rows.astype(BF16))
    normed = layer_norm(rows, gain[...], shift[...]).astype(BF16)
    for j in range(3):
        triple[j] = dot(normed, weights[:, j].reshape(width, -1)).astype(BF16)


def encode(frames, gain, shift, weights):
    length, width = frames.shape
    parts, _, depth, columns = weights.shape
    tile = 512
    padded = round_up(length, tile)
    whole = lambda shape: pl.BlockSpec(shape, lambda i: (0,) * len(shape))
    return pl.pallas_call(
        functools.partial(encode_kernel, length),
        grid=(padded // tile,),
        in_specs=[
            pl.BlockSpec((tile, width), lambda i: (i, 0)),
            whole((1, width)),
            whole((1, width)),
            whole((parts, 3, depth, columns)),
        ],
        out_specs=[
            pl.BlockSpec((3, tile, columns), lambda i: (0, i, 0)),
            pl.BlockSpec((tile // 2, width), lambda i: (i, 0)),
        ],
        out_shape=[
            jax.ShapeDtypeStruct((3, padded, columns), BF16),
            jax.ShapeDtypeStruct((padded // 2, width), F32),
        ],
        compiler_params=params(),
        cost_estimate=pl.CostEstimate(
            flops=6 * padded * width * columns, bytes_accessed=14 * 2**20, transcendentals=0
        ),
        name="encode",
    )(frames, gain[None], shift[None], weights)


def encoder_attention_kernel(count, queries, keys, values, out):
    tile, columns = queries.shape[1:]
    total = keys.shape[1]
    index = lax.broadcasted_iota(jnp.int32, (1, total), 1)
    bias = jnp.where(index < count[0], 0.0, -jnp.inf)
    pairs = pair_matrix(tile)
    for head in range(columns // EHD):
        span = slice(head * EHD, (head + 1) * EHD)
        scores = dot_t(queries[0, :, span], keys[0, :, span]) * (EHD**-0.5 * LOG2E) + bias
        weights = jnp.exp2(scores - jnp.max(scores, -1, keepdims=True))
        total_weight = jnp.sum(weights, -1, keepdims=True)
        context = dot(weights.astype(BF16), values[0, :, span]) / total_weight
        out[:, span] = dot(pairs, context.astype(BF16)).astype(BF16)
    if out.shape[1] > columns:
        out[:, columns:] = jnp.zeros((tile // 2, out.shape[1] - columns), BF16)


def encoder_attention(triple, count):
    _, padded, columns = triple.shape
    tile = 512
    return pl.pallas_call(
        encoder_attention_kernel,
        grid=(padded // tile,),
        in_specs=[
            pl.BlockSpec(memory_space=pltpu.SMEM),
            pl.BlockSpec((1, tile, columns), lambda i: (0, i, 0)),
            pl.BlockSpec((1, padded, columns), lambda i: (1, 0, 0)),
            pl.BlockSpec((1, padded, columns), lambda i: (2, 0, 0)),
        ],
        out_specs=pl.BlockSpec((tile // 2, round_up(columns, 128)), lambda i: (i, 0)),
        out_shape=jax.ShapeDtypeStruct((padded // 2, round_up(columns, 128)), BF16),
        compiler_params=params(),
        cost_estimate=pl.CostEstimate(
            flops=16 * padded * padded * columns,
            bytes_accessed=4 * 2**20,
            transcendentals=padded * padded * (columns // EHD),
        ),
        name="encoder_attention",
    )(count, triple, triple, triple)


def embed_kernel(
    audio, pooled, context_a, context_b, out_a, out_b, gain, shift, a_top, a_end, b_top, b_end,
    proj_shift, text, root_gain, low_w, normed_out, low_out,
):
    tile = pooled.shape[0]
    heads = out_a.shape[0]
    hidden = (
        pooled[...] + dot(context_a[:, :heads], out_a[...]) + dot(context_b[:, :heads], out_b[...])
    )
    pooled_norm = layer_norm(hidden, gain[...], shift[...]).astype(BF16)
    half, columns = a_top.shape
    left, right = pooled_norm[:, :half], pooled_norm[:, half:]
    first = dot(left, a_top[...]) + dot(right, a_end[...]) + proj_shift[:, :columns]
    second = dot(left, b_top[...]) + dot(right, b_end[...]) + proj_shift[:, columns:]
    first, second = first.astype(BF16), second.astype(BF16)
    embedded = jnp.concatenate([first, second], 1).astype(F32)
    index = lax.broadcasted_iota(jnp.int32, (tile, 1), 0) + pl.program_id(0) * tile
    rows = jnp.where(index < audio, embedded, text[...].astype(F32))
    scale = lax.rsqrt(jnp.mean(rows * rows, -1, keepdims=True) + EPS_ROOT)
    normed = (rows * scale * root_gain[...]).astype(BF16)
    normed_out[...] = normed
    low_out[...] = dot(normed, low_w[...]).astype(BF16)


def embed(audio, pooled, context_a, context_b, out_a, out_b, gain, shift, projections,
          proj_shift, text, root_gain, low_w):
    total, features = text.shape
    width = pooled.shape[1]
    tile = total // 2
    last = -(-pooled.shape[0] // tile) - 1
    whole = lambda shape: pl.BlockSpec(shape, lambda i: (0,) * len(shape))
    held = lambda i: (jnp.minimum(i, last), 0)
    row = lambda i: (i, 0)
    return pl.pallas_call(
        functools.partial(embed_kernel, audio),
        grid=(total // tile,),
        in_specs=[
            pl.BlockSpec((tile, width), held),
            pl.BlockSpec((tile, context_a.shape[1]), held),
            pl.BlockSpec((tile, context_b.shape[1]), held),
            whole(out_a.shape),
            whole(out_b.shape),
            whole((1, width)),
            whole((1, width)),
            *[whole(p.shape) for p in projections],
            whole((1, features)),
            pl.BlockSpec((tile, features), row),
            whole((1, features)),
            whole(low_w.shape),
        ],
        out_specs=[
            pl.BlockSpec((tile, features), row),
            pl.BlockSpec((tile, low_w.shape[1]), row),
        ],
        out_shape=[
            jax.ShapeDtypeStruct((total, features), BF16),
            jax.ShapeDtypeStruct((total, low_w.shape[1]), BF16),
        ],
        compiler_params=params(),
        cost_estimate=pl.CostEstimate(
            flops=2 * total * width * features * 2, bytes_accessed=24 * 2**20, transcendentals=0
        ),
        name="embed",
    )(pooled, context_a, context_b, out_a, out_b, gain[None], shift[None], *projections,
      proj_shift[None], text, root_gain[None], low_w)


def decoder_kernel(
    audio, count, normed, low, weights, up_w, upstream, cosine, sine, grads_out, grads_in,
    terms, grad_value,
):
    total, features = normed.shape
    step = pl.program_id(0)
    depth = weights.shape[1] // 3
    columns = weights.shape[2]
    scale = HD**-0.5

    @pl.when(step == 0)
    def _():
        terms[...] = jnp.zeros_like(terms)

    rows = normed[...]
    base = [
        dot(rows, weights[:, j * depth:(j + 1) * depth].reshape(features, columns))
        for j in range(3)
    ]
    up_q = up_w[0].astype(BF16)
    up_v = up_w[1].astype(BF16)
    low_q = low[:, :RANK]
    low_v = low[:, RANK:]
    all_q = base[0] + ADAPTER_SCALE * dot(low_q, up_q)
    all_v = (base[2] + ADAPTER_SCALE * dot(low_v, up_v)).astype(BF16)
    cos_t = cosine[...]
    sin_t = sine[...]
    usable = (count[0] + 1) // 2
    block = 256
    for head in range(columns // HD):
        span = slice(head * HD, (head + 1) * HD)
        q = all_q[:, span]
        k = base[1][:, span]
        q = (q * cos_t + pltpu.roll(q, HD // 2, 1) * sin_t).astype(BF16)
        k = (k * cos_t + pltpu.roll(k, HD // 2, 1) * sin_t).astype(BF16)
        v = all_v[:, span]
        u = upstream[:, span]
        grad_value[...] = jnp.zeros_like(grad_value)
        pieces = []
        for start in range(0, total, block):
            stop = min(start + block, total)
            key = lax.broadcasted_iota(jnp.int32, (stop - start, stop), 1)
            query = lax.broadcasted_iota(jnp.int32, (stop - start, stop), 0) + start
            allowed = (key <= query) & ((key >= audio) | (key < usable))
            scores = dot_t(q[start:stop], k[:stop]) * (scale * LOG2E)
            scores = jnp.where(allowed, scores, -jnp.inf)
            w = jnp.exp2(scores - jnp.max(scores, -1, keepdims=True))
            over = 1.0 / jnp.sum(w, -1, keepdims=True)
            w16 = w.astype(BF16)
            context = (dot(w16, v[:stop]) * over).astype(BF16)
            ub = u[start:stop].astype(F32)
            delta = jnp.sum(ub * context.astype(F32), -1, keepdims=True) * over
            scaled = (ub * over).astype(BF16)
            grad_probs = dot_t(scaled, v[:stop])
            dscores = (w * (grad_probs - delta)).astype(BF16)
            pieces.append(dot(dscores, k[:stop]) * scale)
            grad_value[:stop] += dot_0(w16, scaled)
        gq = jnp.concatenate(pieces, 0)
        gq = (gq * cos_t - pltpu.roll(gq, HD // 2, 1) * sin_t).astype(BF16)
        gv = grad_value[...].astype(BF16)
        grads_out[0, :, span] = ADAPTER_SCALE * dot_0(low_q, gq)
        grads_out[1, :, span] = ADAPTER_SCALE * dot_0(low_v, gv)
        terms[:, :RANK] += dot_t(gq, up_q[:, span])
        terms[:, RANK:] += dot_t(gv, up_v[:, span])

    @pl.when(step == pl.num_programs(0) - 1)
    def _():
        grads_in[...] = ADAPTER_SCALE * dot_0(terms[...].astype(BF16), rows)


def decoder(audio, count, normed, low, weights, up_w, upstream, cosine, sine):
    total, features = normed.shape
    parts, deep, all_columns = weights.shape
    columns = 2 * HD
    whole = lambda shape: pl.BlockSpec(shape, lambda i: (0,) * len(shape))
    return pl.pallas_call(
        functools.partial(decoder_kernel, audio),
        grid=(all_columns // columns,),
        in_specs=[
            pl.BlockSpec(memory_space=pltpu.SMEM),
            whole((total, features)),
            whole((total, 2 * RANK)),
            pl.BlockSpec((parts, deep, columns), lambda i: (0, 0, i)),
            pl.BlockSpec((2, RANK, columns), lambda i: (0, 0, i)),
            pl.BlockSpec((total, columns), lambda i: (0, i)),
            whole((total, HD)),
            whole((total, HD)),
        ],
        out_specs=[
            pl.BlockSpec((2, RANK, columns), lambda i: (0, 0, i)),
            whole((2 * RANK, features)),
        ],
        out_shape=[
            jax.ShapeDtypeStruct((2, RANK, all_columns), F32),
            jax.ShapeDtypeStruct((2 * RANK, features), F32),
        ],
        scratch_shapes=[pltpu.VMEM((total, 2 * RANK), F32), pltpu.VMEM((total, HD), F32)],
        compiler_params=params(),
        cost_estimate=pl.CostEstimate(
            flops=2 * total * features * all_columns * 5,
            bytes_accessed=24 * 2**20,
            transcendentals=total * total * 8,
        ),
        name="decoder",
    )(count, normed, low, weights, up_w, upstream, cosine, sine)


def reduce_kernel(parts, shared, terms, out, landed, mine, theirs, send_sem, recv_sem, pair_sem):
    dp = lax.axis_index("dp")
    tensor = lax.axis_index("tensor")
    partner = (dp, 1 - tensor)
    barrier = pltpu.get_barrier_semaphore()
    for k in range(1, parts):
        pl.semaphore_signal(
            barrier, inc=1, device_id=(lax.rem(dp + k, parts), tensor), device_id_type=MESH
        )
    pl.semaphore_signal(barrier, inc=1, device_id=partner, device_id_type=MESH)
    pl.semaphore_wait(barrier, parts)
    copies = []
    for k in range(1, parts):
        peer = lax.rem(dp + k, parts)
        copy = pltpu.make_async_remote_copy(
            src_ref=terms.at[peer],
            dst_ref=landed.at[k - 1],
            send_sem=send_sem.at[k - 1],
            recv_sem=recv_sem.at[k - 1],
            device_id=(peer, tensor),
            device_id_type=MESH,
        )
        copy.start()
        copies.append(copy)
    total = terms[dp].astype(F32)
    for k, copy in enumerate(copies):
        copy.wait()
        total = total + landed[k].astype(F32)
    mine[...] = total[:shared]
    copy = pltpu.make_async_remote_copy(
        src_ref=mine, dst_ref=theirs, send_sem=pair_sem.at[0], recv_sem=pair_sem.at[1],
        device_id=partner, device_id_type=MESH,
    )
    copy.start()
    out[shared:] = total[shared:]
    copy.wait()
    out[:shared] = total[:shared] + theirs[...]


def reduce_terms(terms, shared):
    parts, rows, columns = terms.shape
    return pl.pallas_call(
        functools.partial(reduce_kernel, parts, shared),
        out_shape=jax.ShapeDtypeStruct((rows, columns), F32),
        in_specs=[pl.BlockSpec(memory_space=pltpu.VMEM)],
        out_specs=pl.BlockSpec(memory_space=pltpu.VMEM),
        scratch_shapes=[
            pltpu.VMEM((parts - 1, rows, columns), BF16),
            pltpu.VMEM((shared, columns), F32),
            pltpu.VMEM((shared, columns), F32),
            pltpu.SemaphoreType.DMA((parts - 1,)),
            pltpu.SemaphoreType.DMA((parts - 1,)),
            pltpu.SemaphoreType.DMA((2,)),
        ],
        compiler_params=pltpu.CompilerParams(
            collective_id=0, has_side_effects=True, vmem_limit_bytes=VMEM_BYTES
        ),
        name="reduce_terms",
    )(terms)


def ring_index(place, parts):
    half = parts // 2
    row = lax.div(place, half)
    step = place - row * half
    core = lax.rem(step, 2)
    level = lax.div(step, 2)
    level = (1 - row) * level + row * (parts // 4 - 1 - level)
    return level * 4 + row * 2 + core


def ring_place(index, parts):
    core = lax.rem(index, 2)
    row = lax.rem(lax.div(index, 2), 2)
    level = lax.div(index, 4)
    level = (1 - row) * level + row * (parts // 4 - 1 - level)
    return row * (parts // 2) + level * 2 + core


def ring_kernel(parts, count, *refs):
    shards, wholes = refs[:count], refs[count:2 * count]
    local_sem, send_sem, recv_sem = refs[2 * count:]
    me = lax.axis_index("dp")
    tensor = lax.axis_index("tensor")
    place = ring_place(me, parts)
    right = ring_index(lax.rem(place + 1, parts), parts)
    left = ring_index(lax.rem(place + parts - 1, parts), parts)
    barrier = pltpu.get_barrier_semaphore()
    for peer in (left, right):
        pl.semaphore_signal(barrier, inc=1, device_id=(peer, tensor), device_id_type=MESH)
    pl.semaphore_wait(barrier, 2)
    own = []
    for i in range(count):
        copy = pltpu.make_async_copy(shards[i], wholes[i].at[me], local_sem.at[i])
        copy.start()
        own.append(copy)
    sent = []
    before = {}
    ways = ((right, parts // 2, parts - 1), (left, parts - 1 - parts // 2, 1))
    for step in range(parts // 2):
        for i in range(count):
            for way, (peer, steps, turn) in enumerate(ways):
                if step >= steps:
                    continue
                if step > 0:
                    before[way, i].wait_recv()
                owner = ring_index(lax.rem(place + step * turn, parts), parts)
                copy = pltpu.make_async_remote_copy(
                    src_ref=shards[i] if step == 0 else wholes[i].at[owner],
                    dst_ref=wholes[i].at[owner],
                    send_sem=send_sem.at[way, step, i],
                    recv_sem=recv_sem.at[way, step, i],
                    device_id=(peer, tensor),
                    device_id_type=MESH,
                )
                copy.start()
                sent.append(copy)
                before[way, i] = copy
    for copy in before.values():
        copy.wait_recv()
    for copy in sent:
        copy.wait_send()
    for copy in own:
        copy.wait()


def ring_gather(shards):
    parts = lax.axis_size("dp")
    count = len(shards)
    anywhere = pl.BlockSpec(memory_space=pl.ANY)
    return pl.pallas_call(
        functools.partial(ring_kernel, parts, count),
        out_shape=[jax.ShapeDtypeStruct((parts,) + s.shape, s.dtype) for s in shards],
        in_specs=[anywhere] * count,
        out_specs=[anywhere] * count,
        scratch_shapes=[
            pltpu.SemaphoreType.DMA((count,)),
            pltpu.SemaphoreType.DMA((2, parts // 2, count)),
            pltpu.SemaphoreType.DMA((2, parts // 2, count)),
        ],
        compiler_params=pltpu.CompilerParams(
            collective_id=1, has_side_effects=True, vmem_limit_bytes=VMEM_BYTES
        ),
        cost_estimate=pl.CostEstimate(flops=0, bytes_accessed=128 * 2**20, transcendentals=0),
        name="ring_gather",
    )(*shards)


def rope_tables(length):
    position = jnp.arange(length).astype(F32)
    frequency = ROPE_BASE ** (-jnp.arange(0, HD, 2).astype(F32) / HD)
    angles = position[:, None] * frequency[None, :]
    cosine, sine = jnp.cos(angles), jnp.sin(angles)
    return jnp.concatenate([cosine, cosine], -1), jnp.concatenate([-sine, sine], -1)


def both(value, axis):
    other = lax.ppermute(value, "tensor", [(0, 1), (1, 0)])
    first = lax.axis_index("tensor") == 0
    return jnp.where(first, value, other), jnp.where(first, other, value)


def swap(value):
    return lax.ppermute(value, "tensor", [(0, 1), (1, 0)])


def other_half(value):
    half = value.shape[0] // 2
    core = lax.rem(lax.axis_index("dp"), 2)
    return swap(lax.dynamic_slice_in_dim(value, core * half, half, 0))


def other_halves(got):
    core = lax.rem(lax.axis_index("dp"), 2)
    mate = lax.ppermute(got, "dp", [(i, i ^ 1) for i in range(lax.axis_size("dp"))])
    return jnp.where(core == 0, got, mate), jnp.where(core == 0, mate, got)


def per_device(
    frames,
    frame_counts,
    encoder_gain,
    encoder_shift,
    encoder_qkv,
    encoder_out,
    post_gain,
    post_shift,
    projector,
    projector_shift,
    text_embed,
    decoder_gain,
    decoder_qkv,
    adapter_in,
    adapter_out,
    audio_upstream,
    text_upstream,
):
    parts = lax.axis_size("dp")
    audio, columns = audio_upstream.shape[1:]
    text_rows = text_upstream.shape[1]
    total = round_up(audio + text_rows, 128)
    tail = total - audio - text_rows
    deep = decoder_qkv.shape[1]

    decoder_w = lax.all_gather(decoder_qkv.reshape(3 * deep, columns), "dp")
    all_frames = jnp.concatenate(both(frames[0], 0), 0)
    shards = [encoder_qkv, encoder_out, projector]
    if parts % 4 == 0 and encoder_qkv.shape[1] % 16 == 0:
        encoder_w, out_parts, proj_parts = ring_gather(shards)
    else:
        encoder_w, out_parts, proj_parts = [lax.all_gather(s, "dp") for s in shards]
        encoder_w = encoder_w.transpose(1, 0, 2, 3).reshape(1, 3, -1, encoder_w.shape[3])
    out_half = out_parts.transpose(1, 0, 2).reshape(encoder_out.shape[0], -1)
    proj = proj_parts.reshape(-1, columns)
    first = lax.axis_index("tensor") == 0
    top, end = proj[: proj.shape[0] // 2], proj[proj.shape[0] // 2:]
    proj_got = other_half(proj)
    out_got = other_half(out_half)
    text = jnp.concatenate(both(text_embed[0], 0), 0)
    text = jnp.pad(text, ((audio, tail), (0, 0)))
    upstream = jnp.pad(
        jnp.concatenate([audio_upstream[0], text_upstream[0]], 0), ((0, tail), (0, 0))
    )
    triple, pooled = encode(all_frames, encoder_gain, encoder_shift, encoder_w)
    context = encoder_attention(triple, frame_counts)
    context, proj_got, out_got = lax.optimization_barrier((context, proj_got, out_got))
    context_other = swap(context)
    other_top, other_end = other_halves(proj_got)
    projections = [
        jnp.where(first, top, other_top),
        jnp.where(first, end, other_end),
        jnp.where(first, other_top, top),
        jnp.where(first, other_end, end),
    ]
    out_other = jnp.concatenate(other_halves(out_got), 0)
    low_w = jnp.concatenate([adapter_in[0], adapter_in[1]], 1).astype(BF16)
    normed, low = embed(
        audio, pooled, context, context_other, out_half, out_other, post_gain, post_shift,
        projections, projector_shift, text, decoder_gain, low_w,
    )
    cosine, sine = rope_tables(total)
    grads_out, grads_in = decoder(
        audio, frame_counts, normed, low, decoder_w, adapter_out, upstream, cosine, sine
    )
    share = grads_in.shape[1] // parts
    ranks = RANK // parts if RANK >= parts else 1
    packed_in = grads_in.reshape(2 * RANK, parts, share).transpose(1, 0, 2)
    packed_out = grads_out.reshape(2, parts, ranks, columns).transpose(1, 0, 2, 3)
    shared = 2 * RANK
    packed = jnp.concatenate(
        [packed_in.astype(BF16), packed_out.astype(BF16).reshape(parts, -1, share)], 1
    )
    summed = reduce_terms(packed, shared)
    half = share // lax.axis_size("tensor")
    part_in = lax.dynamic_slice_in_dim(summed[:shared], lax.axis_index("tensor") * half, half, 1)
    part_in = part_in.reshape(2, RANK, half).transpose(0, 2, 1)
    part_out = summed[shared:].reshape(2, ranks, columns)
    return (part_in, part_out)


def solution(mesh):
    in_specs = (
        P("dp", "tensor", None),
        P("dp"),
        P(),
        P(),
        P(None, "dp", "tensor"),
        P("tensor", "dp"),
        P(),
        P(),
        P("dp", "tensor"),
        P(),
        P("dp", "tensor", None),
        P(),
        P(None, "dp", "tensor"),
        P(),
        P(None, None, "tensor"),
        P("dp", None, "tensor"),
        P("dp", None, "tensor"),
    )
    out_specs = (P(None, ("dp", "tensor"), None), P(None, "dp", "tensor"))
    return jax.shard_map(
        per_device, mesh=mesh, in_specs=in_specs, out_specs=out_specs, check_vma=False
    )
```
